512 devices in a mesh: dp: 32 (over z, x_hi, core), expert: 16 (over x_lo, y).
Axes of the slice: x: 4 (x_hi: 2, x_lo: 2; x = x_hi * 2 + x_lo), y: 8, z: 8, core: 2. Of those that a mesh axis runs over, the one named last changes fastest.
Arguments:
- tokens: bfloat16 [4096, 2048], P('dp'), may hold values from -6 to 6
- out_grad: bfloat16 [4096, 2048], P('dp', 'expert'), may hold values from -6 to 6
- modality: int32 [4096], P('dp'), may hold values 0 or 1
- within_route: int32 [4096], P('dp'), may hold values from 0 to 3
- gate_values: float32 [4096], P('dp'), may hold values from 0.2 to 1
- w_gate: bfloat16 [16, 5504, 2048], P('expert', 'dp'), may hold values from -0.125 to 0.125
- w_up: bfloat16 [16, 5504, 2048], P('expert', 'dp'), may hold values from -0.125 to 0.125
- w_down: bfloat16 [16, 5504, 2048], P('expert', 'dp'), may hold values from -0.0546875 to 0.0546875
Outputs:
- grad_gate: bfloat16 [16, 5504, 2048], P('expert', 'dp')
- grad_up: bfloat16 [16, 5504, 2048], P('expert', 'dp')
- grad_down: bfloat16 [16, 5504, 2048], P('expert', 'dp')
- grad_tokens: bfloat16 [4096, 2048], P('dp', 'expert')
The draws below stay inside these ranges and needn't reach their ends.
All inputs are finite; a program needn't handle non-finite values. No bound on the sum of `modality` on one device may be relied on, other than what follows from the above.
Results may differ from the reference program's by a relative error of at most 0.0058.
Values may be sent and summed in bfloat16 or wider, within the bound.
No kernel may reach another device: no remote copies, remote signals or barrier semaphores. Data moves between devices by JAX's collectives and lax.ppermute only.
A program may use at most 64 MiB of HBM per device.

```python
import jax
import jax.numpy as jnp
from jax import lax

D = 2048
FF = 11008
TOKG = 128
EXPERTS = 8
MOD_EXPERTS = 4
CAP = 24
TOKENS = 4096
N_DP = 32


def with_ends(result, stream_key, smallest, high):
    extent = result.shape
    place = [jax.random.randint(jax.random.fold_in(stream_key, axis), (), 0, extent[axis]) for axis in range(len(extent))]
    result = result.at[tuple(place)].set(smallest)
    longest = extent.index(max(extent))
    place[longest] = (place[longest] + 1) % extent[longest]
    return result.at[tuple(place)].set(high)


def steps_of(stream_key, shape, pieces, least, largest):
    level, own = 1.0, jax.random.fold_in(stream_key, 6)
    for dim, shards_of in pieces:
        steps = jnp.exp(jax.random.uniform(jax.random.fold_in(own, dim), (shards_of,), jnp.float32, least / len(pieces), largest / len(pieces)))
        level = level * jnp.repeat(steps, shape[dim] // shards_of).reshape([-1 if axis == dim else 1 for axis in range(len(shape))])
    return level


def noise(own_key, extent, width, most, shards=(), held_as=jnp.bfloat16):
    array = jax.random.normal(own_key, extent, jnp.float32) * width
    if len(shards) > 0:
        array = steps_of(own_key, extent, shards, -0.22, 0.18) * array
    return jnp.clip(array, min=-most, max=most).astype(held_as)


def setup_inputs(seed: int = 0) -> dict:
    streams_of = jax.random.split(jax.random.key(seed), 9)
    return {
        "tokens": noise(streams_of[0], (TOKENS, D), 1.0, 6.0, ((0, 32),)),
        "out_grad": noise(streams_of[1], (TOKENS, D), 1.0, 6.0, ((0, 32), (1, 16))),
        "modality": with_ends((jax.random.randint(streams_of[2], (TOKENS,), 0, 4) < 3).astype(jnp.int32), jax.random.fold_in(streams_of[2], 1), 0, 1),
        "within_route": with_ends(jax.random.randint(streams_of[3], (TOKENS,), 0, MOD_EXPERTS), jax.random.fold_in(streams_of[3], 1), 0, MOD_EXPERTS - 1).astype(jnp.int32),
        "gate_values": jnp.clip(0.2 + 0.8 * jax.random.uniform(streams_of[4], (TOKENS,), jnp.float32) ** steps_of(streams_of[4], (TOKENS,), ((0, 32),), -0.2, 0.2), 0.2, 1.0),
        "w_gate": noise(streams_of[5], (2 * EXPERTS, FF // 2, D), D ** -0.5, 0.125, ((0, 16), (1, 32))),
        "w_up": noise(streams_of[6], (2 * EXPERTS, FF // 2, D), D ** -0.5, 0.125, ((0, 16), (1, 32))),
        "w_down": noise(streams_of[7], (2 * EXPERTS, FF // 2, D), FF ** -0.5, 0.0546875, ((0, 16), (1, 32))),
    }


def reference(tokens, out_grad, modality, within_route, gate_values, w_gate, w_up, w_down):
    expert_id = (MOD_EXPERTS * modality + within_route).astype(jnp.int32)
    one_hot = (expert_id[:, None] == jnp.arange(EXPERTS, dtype=jnp.int32)[None, :]).astype(jnp.int32)
    grouped = one_hot.reshape(N_DP, TOKG, EXPERTS)
    before = (jnp.cumsum(grouped, axis=1) - grouped).reshape(TOKENS, EXPERTS)
    slot_rank = jnp.sum(before * one_hot, axis=1).astype(jnp.int32)
    group_id = (jnp.arange(TOKENS, dtype=jnp.int32) // TOKG).astype(jnp.int32)
    all_slots = N_DP * EXPERTS * CAP
    dest = jnp.where(slot_rank < CAP, (expert_id * N_DP + group_id) * CAP + slot_rank, all_slots).astype(jnp.int32)
    table = jnp.full((all_slots + 1,), TOKENS, jnp.int32).at[dest].set(jnp.arange(TOKENS, dtype=jnp.int32))
    table = table[:all_slots].reshape(EXPERTS, N_DP * CAP)
    scaled = (gate_values[:, None] * out_grad.astype(jnp.float32)).astype(jnp.bfloat16)
    padded_x = jnp.concatenate([tokens, jnp.zeros((1, D), jnp.bfloat16)], axis=0)
    padded_dy = jnp.concatenate([scaled, jnp.zeros((1, D), jnp.bfloat16)], axis=0)

    def one_expert(k):
        rows = table[k]
        x_rows = padded_x[rows]
        dy_rows = padded_dy[rows]
        wg = jnp.concatenate([w_gate[2 * k], w_gate[2 * k + 1]], axis=0)
        wu = jnp.concatenate([w_up[2 * k], w_up[2 * k + 1]], axis=0)
        wd = jnp.concatenate([w_down[2 * k], w_down[2 * k + 1]], axis=0)
        gate_pre = jnp.dot(x_rows, wg.T, preferred_element_type=jnp.float32)
        up_pre = jnp.dot(x_rows, wu.T, preferred_element_type=jnp.float32)
        sig_gate = jax.nn.sigmoid(gate_pre)
        silu_gate = gate_pre * sig_gate
        hidden = (silu_gate * up_pre).astype(jnp.bfloat16)
        d_hidden = jnp.dot(dy_rows, wd.T, preferred_element_type=jnp.float32)
        d_gate = (d_hidden * up_pre * sig_gate * (1.0 + gate_pre * (1.0 - sig_gate))).astype(jnp.bfloat16)
        d_up = (d_hidden * silu_gate).astype(jnp.bfloat16)
        grad_g = jnp.dot(d_gate.T, x_rows, preferred_element_type=jnp.float32).astype(jnp.bfloat16)
        grad_u = jnp.dot(d_up.T, x_rows, preferred_element_type=jnp.float32).astype(jnp.bfloat16)
        grad_d = jnp.dot(hidden.T, dy_rows, preferred_element_type=jnp.float32).astype(jnp.bfloat16)
        dx_rows = jnp.dot(d_gate, wg, preferred_element_type=jnp.float32) + jnp.dot(d_up, wu, preferred_element_type=jnp.float32)
        return grad_g, grad_u, grad_d, dx_rows

    grad_g, grad_u, grad_d, dx_rows = lax.map(one_expert, jnp.arange(EXPERTS, dtype=jnp.int32))
    half = FF // 2
    grad_gate = grad_g.reshape(2 * EXPERTS, half, D)
    grad_up = grad_u.reshape(2 * EXPERTS, half, D)
    grad_down = grad_d.reshape(2 * EXPERTS, half, D)
    summed = jnp.zeros((TOKENS + 1, D), jnp.float32).at[table.reshape(-1)].add(dx_rows.reshape(-1, D))
    grad_tokens = summed[:TOKENS].astype(jnp.bfloat16)
    return grad_gate, grad_up, grad_down, grad_tokens
```

```python
import jax
import jax.numpy as jnp
from jax import lax
from jax.sharding import Mesh
from jax.sharding import PartitionSpec as P

BF = jnp.bfloat16
F32 = jnp.float32
Z, XH, CORE, XL, Y = 8, 2, 2, 2, 8
AXES = ("z", "xh", "core", "xl", "y")
EXPERT = ("xl", "y")
SWAP = [(0, 1), (1, 0)]
CROSS = [(0, 3), (1, 2), (2, 1), (3, 0)]
ONWARD = [(2 * z + c, 2 * ((z + 1 - 2 * c) % Z) + c) for z in range(Z) for c in range(2)]
HOMEWARD = [(b, a) for a, b in ONWARD]
PAD = 176


def dot(a, b, dims=((1,), (0,))):
    return lax.dot_general(a, b, (dims, ((), ())), preferred_element_type=F32)


def onward(a):
    return lax.ppermute(a, ("z", "core"), ONWARD)


def homeward(a):
    return lax.ppermute(a, ("z", "core"), HOMEWARD)


def plane_rows(a):
    return jnp.concatenate(
        [
            a,
            lax.ppermute(a, "xh", SWAP),
            lax.ppermute(a, "core", SWAP),
            lax.ppermute(a, ("xh", "core"), CROSS),
        ],
        axis=0,
    )


def ring_rows(rows):
    half = rows.shape[0] // 2
    one = onward(rows)
    two = onward(one)
    three = onward(two)
    four = onward(three[:half])
    return [rows[:half], one, two, three, four]


def local(tokens, out_grad, modality, within_route, gate_values, w_gate, w_up, w_down):
    tok_count, width = tokens.shape
    experts_all = XL * Y // 2
    per_modality = experts_all // 2
    capacity = tok_count * 3 // (2 * experts_all)
    hidden_own = w_gate.shape[1]
    position = lax.axis_index(EXPERT)
    own_expert = position // 2
    expert_id = per_modality * modality + within_route
    one_hot = (expert_id[:, None] == jnp.arange(experts_all, dtype=jnp.int32)[None, :]).astype(
        jnp.int32
    )
    before = jnp.cumsum(one_hot, axis=0) - one_hot
    slot_rank = jnp.sum(before * one_hot, axis=1)
    kept = slot_rank < capacity
    slot = jnp.where(kept, expert_id * capacity + slot_rank, -1)
    slots = jnp.arange(experts_all * capacity, dtype=jnp.int32)
    select = (slot[None, :] == slots[:, None]).astype(BF)
    own_slots = own_expert * capacity + jnp.arange(capacity, dtype=jnp.int32)
    select_own = (slot[None, :] == own_slots[:, None]).astype(BF)

    pad = ((0, PAD - hidden_own), (0, 0))
    own_w = jnp.stack([jnp.pad(w_gate[0], pad), jnp.pad(w_up[0], pad), jnp.pad(w_down[0], pad)])
    other_w = lax.ppermute(own_w, "core", SWAP)
    wg = jnp.concatenate([own_w[0], other_w[0]], axis=0)
    wu = jnp.concatenate([own_w[1], other_w[1]], axis=0)
    wd = jnp.concatenate([own_w[2], other_w[2]], axis=0)

    x_own = dot(select_own, tokens).astype(BF)
    x_plane, wg, wu, wd = lax.optimization_barrier((plane_rows(x_own), wg, wu, wd))
    x_parts = ring_rows(x_plane)
    scaled = (gate_values[:, None] * out_grad.astype(F32)).astype(BF)
    dy_slices = dot(select, scaled).astype(BF).reshape(experts_all, 1, capacity, -1)
    dy_slices = jnp.broadcast_to(dy_slices, (experts_all, 2) + dy_slices.shape[2:])
    dy_slices = dy_slices.reshape((2 * experts_all,) + dy_slices.shape[2:])
    dy_slices = lax.all_to_all(dy_slices, EXPERT, 0, 0, tiled=True)
    dy_own = jnp.transpose(dy_slices, (1, 0, 2)).reshape(capacity, width)
    dy_parts = ring_rows(plane_rows(dy_own))

    cols = ((1,), (1,))
    terms, hiddens, d_gates, d_ups = [], [], [], []
    for x_rows, dy_rows in zip(x_parts, dy_parts):
        gate_pre = dot(x_rows, wg, cols)
        up_pre = dot(x_rows, wu, cols)
        sig_gate = jax.nn.sigmoid(gate_pre)
        silu_gate = gate_pre * sig_gate
        hiddens.append((silu_gate * up_pre).astype(BF))
        d_hidden = dot(dy_rows, wd, cols)
        d_gate = (d_hidden * up_pre * sig_gate * (1.0 + gate_pre * (1.0 - sig_gate))).astype(BF)
        d_up = (d_hidden * silu_gate).astype(BF)
        d_gates.append(d_gate)
        d_ups.append(d_up)
        terms.append(dot(d_gate, wg) + dot(d_up, wu))

    half = terms[0].shape[0]
    travelling = homeward(terms[4].astype(BF)).astype(F32)
    travelling = jnp.concatenate([terms[3][:half] + travelling, terms[3][half:]], axis=0)
    travelling = homeward(travelling.astype(BF)).astype(F32)
    travelling = homeward((terms[2] + travelling).astype(BF)).astype(F32)
    travelling = homeward((terms[1] + travelling).astype(BF)).astype(F32)
    across = lax.ppermute(travelling[half:].astype(BF), "core", SWAP).astype(F32)
    travelling = terms[0] + travelling[:half] + across
    across = lax.ppermute(travelling[capacity:].astype(BF), "xh", SWAP).astype(F32)
    summed = (travelling[:capacity] + across).reshape(capacity, 2 * experts_all, -1)
    summed = jnp.transpose(summed, (1, 0, 2)).astype(BF)
    summed = lax.all_to_all(summed, EXPERT, 0, 0, tiled=True)

    from_slots = jnp.arange(2 * experts_all * capacity, dtype=jnp.int32)
    from_slots = from_slots // (2 * capacity) * capacity + from_slots % capacity
    place = (slot[:, None] == from_slots[None, :]).astype(BF)
    grad_tokens = dot(place, summed.reshape(2 * experts_all * capacity, -1)).astype(BF)

    x_all = jnp.concatenate(x_parts, axis=0)
    dy_all = jnp.concatenate(dy_parts, axis=0)
    rows = ((0,), (0,))
    grads = [
        dot(jnp.concatenate(d_gates, axis=0), x_all, rows),
        dot(jnp.concatenate(d_ups, axis=0), x_all, rows),
        dot(jnp.concatenate(hiddens, axis=0), dy_all, rows),
    ]
    outs = []
    for grad in grads:
        received = lax.ppermute(grad[PAD:].astype(BF), "core", SWAP).astype(F32)
        outs.append((grad[:PAD] + received)[:hidden_own].astype(BF)[None])
    return (*outs, grad_tokens)


def solution(mesh):
    fine = Mesh(mesh.devices.reshape(Z, XH, CORE, XL, Y), AXES)
    dp = ("z", "xh", "core")
    placed = (
        P(dp, None),
        P(dp, EXPERT),
        P(dp),
        P(dp),
        P(dp),
        P(EXPERT, dp, None),
        P(EXPERT, dp, None),
        P(EXPERT, dp, None),
    )
    return jax.shard_map(
        local,
        mesh=fine,
        in_specs=placed,
        out_specs=(
            P(EXPERT, dp, None),
            P(EXPERT, dp, None),
            P(EXPERT, dp, None),
            P(dp, EXPERT),
        ),
        check_vma=False,
    )
```

```python
import jax
import jax.numpy as jnp
from jax import lax
from jax.sharding import Mesh
from jax.sharding import PartitionSpec as P

BF = jnp.bfloat16
F32 = jnp.float32
Z, XH, CORE, XL, Y = 8, 2, 2, 2, 8
AXES = ("z", "xh", "core", "xl", "y")
EXPERT = ("xl", "y")
PLANE = ("z", "xh", "core")
PAD = 176


def hops(step, across=False, other=False):
    pairs = []
    for z in range(Z):
        for x in range(XH):
            for c in range(CORE):
                there = ((z + step * (1 - 2 * c)) % Z, x ^ across, c ^ other)
                pairs.append(((z * XH + x) * CORE + c, (there[0] * XH + there[1]) * CORE + there[2]))
    return pairs


def send(a, step, across=False, other=False):
    return lax.ppermute(a, PLANE, hops(step, across, other))


def dot(a, b, dims=((1,), (0,))):
    return lax.dot_general(a, b, (dims, ((), ())), preferred_element_type=F32)


def local(tokens, out_grad, modality, within_route, gate_values, w_gate, w_up, w_down):
    tok_count, width = tokens.shape
    experts_all = XL * Y // 2
    per_modality = experts_all // 2
    capacity = tok_count * 3 // (2 * experts_all)
    hidden_own = w_gate.shape[1]
    position = lax.axis_index(EXPERT)
    own_expert = position // 2
    expert_id = per_modality * modality + within_route
    one_hot = (expert_id[:, None] == jnp.arange(experts_all, dtype=jnp.int32)[None, :]).astype(
        jnp.int32
    )
    before = jnp.cumsum(one_hot, axis=0) - one_hot
    slot_rank = jnp.sum(before * one_hot, axis=1)
    kept = slot_rank < capacity
    slot = jnp.where(kept, expert_id * capacity + slot_rank, -1)
    slots = jnp.arange(experts_all * capacity, dtype=jnp.int32)
    select = (slot[None, :] == slots[:, None]).astype(BF)
    own_slots = own_expert * capacity + jnp.arange(capacity, dtype=jnp.int32)
    select_own = (slot[None, :] == own_slots[:, None]).astype(BF)

    pad = ((0, PAD - hidden_own), (0, 0))
    own_w = jnp.stack([jnp.pad(w_gate[0], pad), jnp.pad(w_up[0], pad), jnp.pad(w_down[0], pad)])
    other_w = send(own_w, 0, other=True)
    wg = jnp.concatenate([own_w[0], other_w[0]], axis=0)
    wu = jnp.concatenate([own_w[1], other_w[1]], axis=0)
    wd = jnp.concatenate([own_w[2], other_w[2]], axis=0)

    scaled = (gate_values[:, None] * out_grad.astype(F32)).astype(BF)
    dy_slices = dot(select, scaled).astype(BF).reshape(experts_all, 1, capacity, -1)
    dy_slices = jnp.broadcast_to(dy_slices, (experts_all, 2) + dy_slices.shape[2:])
    dy_slices = dy_slices.reshape((2 * experts_all,) + dy_slices.shape[2:])
    dy_slices = lax.all_to_all(dy_slices, EXPERT, 0, 0, tiled=True)
    x_own = dot(select_own, tokens).astype(BF)
    dy_own = jnp.transpose(dy_slices, (1, 0, 2)).reshape(capacity, width)
    own = jnp.concatenate([x_own, dy_own], axis=0)
    across = send(own, 0, across=True)

    near = 2 * capacity
    packet = jnp.concatenate(
        [own[:capacity], across[:capacity], own[capacity:], across[capacity:]], axis=0
    )
    packet = packet + other_w[2, hidden_own, 0]
    chain_a = [send(packet, 1)]
    chain_b = [send(packet, -1, other=True)]
    for step in (1, 2):
        chain_a.append(send(chain_a[-1], 1))
        chain_b.append(send(chain_b[-1], 1))
    chain_a.append(send(chain_a[-1], 1))
    chunks = [(packet[:near], packet[near:])]
    for a, b in zip(chain_a[:3], chain_b):
        chunks.append(
            (
                jnp.concatenate([a[:near], b[:near]], axis=0),
                jnp.concatenate([a[near:], b[near:]], axis=0),
            )
        )
    chunks.append((chain_a[3][:near], chain_a[3][near:]))

    cols = ((1,), (1,))
    terms, hiddens, d_gates, d_ups = [], [], [], []
    for x_rows, dy_rows in chunks:
        gate_pre = dot(x_rows, wg, cols)
        up_pre = dot(x_rows, wu, cols)
        sig_gate = jax.nn.sigmoid(gate_pre)
        silu_gate = gate_pre * sig_gate
        hiddens.append((silu_gate * up_pre).astype(BF))
        d_hidden = dot(dy_rows, wd, cols)
        d_gate = (d_hidden * up_pre * sig_gate * (1.0 + gate_pre * (1.0 - sig_gate))).astype(BF)
        d_up = (d_hidden * silu_gate).astype(BF)
        d_gates.append(d_gate)
        d_ups.append(d_up)
        terms.append(dot(d_gate, wg) + dot(d_up, wu))

    x_all = jnp.concatenate([x for x, _ in chunks], axis=0)
    dy_all = jnp.concatenate([dy for _, dy in chunks], axis=0)
    rows = ((0,), (0,))
    grads = [
        dot(jnp.concatenate(d_gates, axis=0), x_all, rows),
        dot(jnp.concatenate(d_ups, axis=0), x_all, rows),
        dot(jnp.concatenate(hiddens, axis=0), dy_all, rows),
    ]
    received = send(jnp.stack([grad[PAD:].astype(BF) for grad in grads]), 0, other=True)

    home_b = terms[3][near:]
    home_b = terms[2][near:] + send(home_b.astype(BF), -1).astype(F32)
    home_b = (terms[1][near:] + send(home_b.astype(BF), -1).astype(F32)).astype(BF)
    home_a = terms[4]
    home_a = terms[3][:near] + send(home_a.astype(BF), -1).astype(F32)
    home_a = terms[2][:near] + send(home_a.astype(BF), -1).astype(F32)
    home_a = (terms[1][:near] + send(home_a.astype(BF), -1).astype(F32)).astype(BF)
    summed = terms[0][:capacity]
    summed = summed + send(terms[0][capacity:].astype(BF), 0, across=True).astype(F32)
    summed = summed + send(home_b[:capacity], -1, other=True).astype(F32)
    summed = summed + send(home_b[capacity:], -1, across=True, other=True).astype(F32)
    summed = summed + send(home_a[:capacity], -1).astype(F32)
    summed = summed + send(home_a[capacity:], -1, across=True).astype(F32)
    summed = summed + received[2, hidden_own, 0].astype(F32)
    summed = summed.reshape(capacity, 2 * experts_all, -1)
    summed = jnp.transpose(summed, (1, 0, 2)).astype(BF)
    summed = lax.all_to_all(summed, EXPERT, 0, 0, tiled=True)

    from_slots = jnp.arange(2 * experts_all * capacity, dtype=jnp.int32)
    from_slots = from_slots // (2 * capacity) * capacity + from_slots % capacity
    place = (slot[:, None] == from_slots[None, :]).astype(BF)
    grad_tokens = dot(place, summed.reshape(2 * experts_all * capacity, -1)).astype(BF)

    outs = [
        (grad[:PAD] + extra.astype(F32))[:hidden_own].astype(BF)[None]
        for grad, extra in zip(grads, received)
    ]
    return (*outs, grad_tokens)


def solution(mesh):
    fine = Mesh(mesh.devices.reshape(Z, XH, CORE, XL, Y), AXES)
    dp = ("z", "xh", "core")
    placed = (
        P(dp, None),
        P(dp, EXPERT),
        P(dp),
        P(dp),
        P(dp),
        P(EXPERT, dp, None),
        P(EXPERT, dp, None),
        P(EXPERT, dp, None),
    )
    return jax.shard_map(
        local,
        mesh=fine,
        in_specs=placed,
        out_specs=(
            P(EXPERT, dp, None),
            P(EXPERT, dp, None),
            P(EXPERT, dp, None),
            P(dp, EXPERT),
        ),
        check_vma=False,
    )
```

```python
import jax
import jax.numpy as jnp
from jax import lax
from jax.sharding import Mesh
from jax.sharding import PartitionSpec as P

BF = jnp.bfloat16
F32 = jnp.float32
Z, XH, CORE, XL, Y = 8, 2, 2, 2, 8
AXES = ("z", "xh", "core", "xl", "y")
EXPERT = ("xl", "y")
PLANE = ("z", "xh", "core")
PAD = 176


def hops(step, across=False, other=False):
    pairs = []
    for z in range(Z):
        for x in range(XH):
            for c in range(CORE):
                there = ((z + step * (1 - 2 * c)) % Z, x ^ across, c ^ other)
                pairs.append(((z * XH + x) * CORE + c, (there[0] * XH + there[1]) * CORE + there[2]))
    return pairs


def send(a, step, across=False, other=False):
    return lax.ppermute(a, PLANE, hops(step, across, other))


def dot(a, b, dims=((1,), (0,))):
    return lax.dot_general(a, b, (dims, ((), ())), preferred_element_type=F32)


def after(a, *earlier):
    for b in earlier:
        a = a + (b[:1] * 0).astype(a.dtype)
    return a


def local(tokens, out_grad, modality, within_route, gate_values, w_gate, w_up, w_down):
    tok_count, width = tokens.shape
    experts_all = XL * Y // 2
    per_modality = experts_all // 2
    capacity = tok_count * 3 // (2 * experts_all)
    hidden_own = w_gate.shape[1]
    position = lax.axis_index(EXPERT)
    own_expert = position // 2
    expert_id = per_modality * modality + within_route
    one_hot = (expert_id[:, None] == jnp.arange(experts_all, dtype=jnp.int32)[None, :]).astype(
        jnp.int32
    )
    before = jnp.cumsum(one_hot, axis=0) - one_hot
    slot_rank = jnp.sum(before * one_hot, axis=1)
    kept = slot_rank < capacity
    slot = jnp.where(kept, expert_id * capacity + slot_rank, -1)
    slots = jnp.arange(experts_all * capacity, dtype=jnp.int32)
    select = (slot[None, :] == slots[:, None]).astype(BF)
    own_slots = own_expert * capacity + jnp.arange(capacity, dtype=jnp.int32)
    select_own = (slot[None, :] == own_slots[:, None]).astype(BF)

    pad = ((0, PAD - hidden_own), (0, 0))
    own_w = jnp.stack([jnp.pad(w_gate[0], pad), jnp.pad(w_up[0], pad), jnp.pad(w_down[0], pad)])
    other_w = send(own_w, 0, other=True)
    wg = jnp.concatenate([own_w[0], other_w[0]], axis=0)
    wu = jnp.concatenate([own_w[1], other_w[1]], axis=0)
    wd = jnp.concatenate([own_w[2], other_w[2]], axis=0)

    near = 2 * capacity
    x_own = dot(select_own, tokens).astype(BF)
    x_across = send(x_own, 0, across=True)
    x0 = jnp.concatenate([x_own, x_across], axis=0)
    x1_a, x1_b = send(x0, 1), send(x0, -1, other=True)
    x1 = jnp.concatenate([x1_a, x1_b], axis=0)
    x2 = send(x1, 1)
    x3 = send(x2, 1)
    x4 = send(x3[:near], 1)

    scaled = (gate_values[:, None] * out_grad.astype(F32)).astype(BF)
    dy_slices = dot(select, scaled).astype(BF).reshape(experts_all, 1, capacity, -1)
    dy_slices = jnp.broadcast_to(dy_slices, (experts_all, 2) + dy_slices.shape[2:])
    dy_slices = dy_slices.reshape((2 * experts_all,) + dy_slices.shape[2:])
    dy_slices = lax.all_to_all(dy_slices, EXPERT, 0, 0, tiled=True)
    dy_own = after(jnp.transpose(dy_slices, (1, 0, 2)).reshape(capacity, width), x_across)
    dy0 = jnp.concatenate([dy_own, send(dy_own, 0, across=True)], axis=0)
    dy0 = after(dy0, x1_a, x1_b)
    dy1 = jnp.concatenate([send(dy0, 1), send(dy0, -1, other=True)], axis=0)
    dy1 = after(dy1, x2, other_w[2])
    dy2 = after(send(dy1, 1), x3)
    dy3 = send(dy2, 1)
    dy4 = send(after(dy3[:near], x4), 1)
    chunks = [(x0, dy0), (x1, dy1), (x2, dy2), (x3, dy3), (x4, dy4)]

    cols = ((1,), (1,))
    terms, hiddens, d_gates, d_ups = [], [], [], []
    for x_rows, dy_rows in chunks:
        gate_pre = dot(x_rows, wg, cols)
        up_pre = dot(x_rows, wu, cols)
        sig_gate = jax.nn.sigmoid(gate_pre)
        silu_gate = gate_pre * sig_gate
        hiddens.append((silu_gate * up_pre).astype(BF))
        d_hidden = dot(dy_rows, wd, cols)
        d_gate = (d_hidden * up_pre * sig_gate * (1.0 + gate_pre * (1.0 - sig_gate))).astype(BF)
        d_up = (d_hidden * silu_gate).astype(BF)
        d_gates.append(d_gate)
        d_ups.append(d_up)
        terms.append(dot(d_gate, wg) + dot(d_up, wu))

    x_all = jnp.concatenate([x for x, _ in chunks], axis=0)
    dy_all = jnp.concatenate([dy for _, dy in chunks], axis=0)
    rows = ((0,), (0,))
    grads = [
        dot(jnp.concatenate(d_gates, axis=0), x_all, rows),
        dot(jnp.concatenate(d_ups, axis=0), x_all, rows),
        dot(jnp.concatenate(hiddens, axis=0), dy_all, rows),
    ]
    received = send(jnp.stack([grad[PAD:].astype(BF) for grad in grads]), 0, other=True)

    came_b = send(terms[3][near:].astype(BF), -1)
    came_a = send(terms[4].astype(BF), -1)
    home_b = terms[2][near:] + came_b.astype(F32)
    home_a = after(terms[3][:near] + came_a.astype(F32), came_b)
    came_b = send(home_b.astype(BF), -1)
    came_a = send(home_a.astype(BF), -1)
    home_b = (terms[1][near:] + came_b.astype(F32)).astype(BF)
    home_a = after(terms[2][:near] + came_a.astype(F32), came_b)
    last_b = [
        send(home_b[:capacity], -1, other=True),
        send(home_b[capacity:], -1, across=True, other=True),
    ]
    came_a = send(home_a.astype(BF), -1)
    home_a = after((terms[1][:near] + came_a.astype(F32)).astype(BF), *last_b)
    last_a = [send(home_a[:capacity], -1), send(home_a[capacity:], -1, across=True)]
    last_0 = send(terms[0][capacity:].astype(BF), 0, across=True)
    summed = terms[0][:capacity]
    for came in (last_0, *last_b, *last_a):
        summed = summed + came.astype(F32)
    summed = summed + received[2, hidden_own, 0].astype(F32)
    summed = summed.reshape(capacity, 2 * experts_all, -1)
    summed = jnp.transpose(summed, (1, 0, 2)).astype(BF)
    summed = lax.all_to_all(summed, EXPERT, 0, 0, tiled=True)

    from_slots = jnp.arange(2 * experts_all * capacity, dtype=jnp.int32)
    from_slots = from_slots // (2 * capacity) * capacity + from_slots % capacity
    place = (slot[:, None] == from_slots[None, :]).astype(BF)
    grad_tokens = dot(place, summed.reshape(2 * experts_all * capacity, -1)).astype(BF)

    outs = [
        (grad[:PAD] + extra.astype(F32))[:hidden_own].astype(BF)[None]
        for grad, extra in zip(grads, received)
    ]
    return (*outs, grad_tokens)


def solution(mesh):
    fine = Mesh(mesh.devices.reshape(Z, XH, CORE, XL, Y), AXES)
    dp = ("z", "xh", "core")
    placed = (
        P(dp, None),
        P(dp, EXPERT),
        P(dp),
        P(dp),
        P(dp),
        P(EXPERT, dp, None),
        P(EXPERT, dp, None),
        P(EXPERT, dp, None),
    )
    return jax.shard_map(
        local,
        mesh=fine,
        in_specs=placed,
        out_specs=(
            P(EXPERT, dp, None),
            P(EXPERT, dp, None),
            P(EXPERT, dp, None),
            P(dp, EXPERT),
        ),
        check_vma=False,
    )
```

```python
import jax
import jax.numpy as jnp
from jax import lax
from jax.sharding import Mesh
from jax.sharding import PartitionSpec as P

BF = jnp.bfloat16
F32 = jnp.float32
Z, XH, CORE, XL, Y = 8, 2, 2, 2, 8
AXES = ("z", "xh", "core", "xl", "y")
EXPERT = ("xl", "y")
PAD = 176
SWAP = [(0, 1), (1, 0)]


def dot(a, b, dims=((1,), (0,))):
    return lax.dot_general(a, b, (dims, ((), ())), preferred_element_type=F32)


def local(tokens, out_grad, modality, within_route, gate_values, w_gate, w_up, w_down):
    tok_count, width = tokens.shape
    experts_all = XL * Y // 2
    per_modality = experts_all // 2
    capacity = tok_count * 3 // (2 * experts_all)
    hidden_own = w_gate.shape[1]
    position = lax.axis_index(EXPERT)
    own_expert = position // 2
    expert_id = per_modality * modality + within_route
    one_hot = (expert_id[:, None] == jnp.arange(experts_all, dtype=jnp.int32)[None, :]).astype(
        jnp.int32
    )
    before = jnp.cumsum(one_hot, axis=0) - one_hot
    slot_rank = jnp.sum(before * one_hot, axis=1)
    kept = slot_rank < capacity
    slot = jnp.where(kept, expert_id * capacity + slot_rank, -1)
    slots = jnp.arange(experts_all * capacity, dtype=jnp.int32)
    select = (slot[None, :] == slots[:, None]).astype(BF)
    own_slots = own_expert * capacity + jnp.arange(capacity, dtype=jnp.int32)
    select_own = (slot[None, :] == own_slots[:, None]).astype(BF)

    pad = ((0, PAD - hidden_own), (0, 0))
    own_w = jnp.stack([jnp.pad(w_gate[0], pad), jnp.pad(w_up[0], pad), jnp.pad(w_down[0], pad)])
    other_w = lax.ppermute(own_w, "core", SWAP)
    wg = jnp.concatenate([own_w[0], other_w[0]], axis=0)
    wu = jnp.concatenate([own_w[1], other_w[1]], axis=0)
    wd = jnp.concatenate([own_w[2], other_w[2]], axis=0)

    x_own = dot(select_own, tokens).astype(BF)
    x_across = lax.ppermute(x_own, "xh", SWAP)
    scaled = (gate_values[:, None] * out_grad.astype(F32)).astype(BF)
    dy_slices = dot(select, scaled).astype(BF).reshape(1, experts_all, 1, capacity, -1)
    dy_slices = jnp.broadcast_to(dy_slices, (XH, experts_all, 2) + dy_slices.shape[3:])
    dy_slices = dy_slices.reshape((XH * XL * Y,) + dy_slices.shape[3:])
    dy_slices = lax.all_to_all(dy_slices, ("xh",) + EXPERT, 0, 0, tiled=True)
    dy_slices = dy_slices.reshape((XH, XL * Y) + dy_slices.shape[1:])
    dy_near = jnp.transpose(dy_slices, (0, 2, 1, 3)).reshape(2 * capacity, width)
    side = lax.axis_index("xh")
    x_near = jnp.concatenate(
        [jnp.where(side == 0, x_own, x_across), jnp.where(side == 0, x_across, x_own)], axis=0
    )
    packet = jnp.concatenate([x_near, dy_near], axis=1)

    packets = lax.all_gather(packet, "z", axis=0, tiled=True)
    x_rows, dy_rows = packets[:, :width], packets[:, width:]
    cols = ((1,), (1,))
    gate_pre = dot(x_rows, wg, cols)
    up_pre = dot(x_rows, wu, cols)
    sig_gate = jax.nn.sigmoid(gate_pre)
    silu_gate = gate_pre * sig_gate
    hidden = (silu_gate * up_pre).astype(BF)
    d_hidden = dot(dy_rows, wd, cols)
    d_gate = (d_hidden * up_pre * sig_gate * (1.0 + gate_pre * (1.0 - sig_gate))).astype(BF)
    d_up = (d_hidden * silu_gate).astype(BF)
    terms = (dot(d_gate, wg) + dot(d_up, wu)).reshape(Z, 2, capacity, width)

    other_terms = lax.dynamic_index_in_dim(terms, 1 - side, axis=1, keepdims=False)
    own_terms = lax.dynamic_index_in_dim(terms, side, axis=1, keepdims=False)
    came = lax.ppermute(other_terms.astype(BF), "xh", SWAP)
    terms = (own_terms + came.astype(F32)).astype(BF)
    terms = lax.all_to_all(terms, "z", 0, 0, tiled=True)
    summed = jnp.sum(terms.astype(F32), axis=0).reshape(capacity, XL * Y, -1)
    summed = jnp.transpose(summed, (1, 0, 2)).astype(BF)
    summed = lax.all_to_all(summed, EXPERT, 0, 0, tiled=True)

    from_slots = jnp.arange(2 * experts_all * capacity, dtype=jnp.int32)
    from_slots = from_slots // (2 * capacity) * capacity + from_slots % capacity
    place = (slot[:, None] == from_slots[None, :]).astype(BF)
    grad_tokens = dot(place, summed.reshape(2 * experts_all * capacity, -1)).astype(BF)

    rows = ((0,), (0,))
    grads = [dot(d_gate, x_rows, rows), dot(d_up, x_rows, rows), dot(hidden, dy_rows, rows)]
    received = lax.ppermute(jnp.stack([grad[PAD:].astype(BF) for grad in grads]), "core", SWAP)
    outs = [
        (grad[:PAD] + extra.astype(F32))[:hidden_own].astype(BF)[None]
        for grad, extra in zip(grads, received)
    ]
    return (*outs, grad_tokens)


def solution(mesh):
    fine = Mesh(mesh.devices.reshape(Z, XH, CORE, XL, Y), AXES)
    dp = ("z", "xh", "core")
    placed = (
        P(dp, None),
        P(dp, EXPERT),
        P(dp),
        P(dp),
        P(dp),
        P(EXPERT, dp, None),
        P(EXPERT, dp, None),
        P(EXPERT, dp, None),
    )
    return jax.shard_map(
        local,
        mesh=fine,
        in_specs=placed,
        out_specs=(
            P(EXPERT, dp, None),
            P(EXPERT, dp, None),
            P(EXPERT, dp, None),
            P(dp, EXPERT),
        ),
        check_vma=False,
    )
```

```python
import jax
import jax.numpy as jnp
from jax import lax
from jax.sharding import Mesh
from jax.sharding import PartitionSpec as P

BF = jnp.bfloat16
F32 = jnp.float32
Z, XH, CORE, XL, Y = 8, 2, 2, 2, 8
AXES = ("z", "xh", "core", "xl", "y")
EXPERT = ("xl", "y")
PAD = 176
SWAP = [(0, 1), (1, 0)]


def ring(a, step, cross=False):
    pairs = []
    for z in range(Z):
        for c in range(CORE):
            up = step * (1 - 2 * c) * (-1 if cross and step == 1 else 1)
            pairs.append((z * CORE + c, (z + up) % Z * CORE + (c ^ cross)))
    return lax.ppermute(a, ("z", "core"), pairs)


def dot(a, b, dims=((1,), (0,))):
    return lax.dot_general(a, b, (dims, ((), ())), preferred_element_type=F32)


def local(tokens, out_grad, modality, within_route, gate_values, w_gate, w_up, w_down):
    tok_count, width = tokens.shape
    experts_all = XL * Y // 2
    per_modality = experts_all // 2
    capacity = tok_count * 3 // (2 * experts_all)
    hidden_own = w_gate.shape[1]
    position = lax.axis_index(EXPERT)
    own_expert = position // 2
    expert_id = per_modality * modality + within_route
    one_hot = (expert_id[:, None] == jnp.arange(experts_all, dtype=jnp.int32)[None, :]).astype(
        jnp.int32
    )
    before = jnp.cumsum(one_hot, axis=0) - one_hot
    slot_rank = jnp.sum(before * one_hot, axis=1)
    kept = slot_rank < capacity
    slot = jnp.where(kept, expert_id * capacity + slot_rank, -1)
    slots = jnp.arange(experts_all * capacity, dtype=jnp.int32)
    select = (slot[None, :] == slots[:, None]).astype(BF)
    own_slots = own_expert * capacity + jnp.arange(capacity, dtype=jnp.int32)
    select_own = (slot[None, :] == own_slots[:, None]).astype(BF)

    pad = ((0, PAD - hidden_own), (0, 0))
    own_w = jnp.stack([jnp.pad(w_gate[0], pad), jnp.pad(w_up[0], pad), jnp.pad(w_down[0], pad)])
    other_w = lax.ppermute(own_w, "core", SWAP)
    wg = jnp.concatenate([own_w[0], other_w[0]], axis=0)
    wu = jnp.concatenate([own_w[1], other_w[1]], axis=0)
    wd = jnp.concatenate([own_w[2], other_w[2]], axis=0)

    x_own = dot(select_own, tokens).astype(BF)
    x_across = lax.ppermute(x_own, "xh", SWAP)
    scaled = (gate_values[:, None] * out_grad.astype(F32)).astype(BF)
    dy_slices = dot(select, scaled).astype(BF).reshape(1, experts_all, 1, capacity, -1)
    dy_slices = jnp.broadcast_to(dy_slices, (XH, experts_all, 2) + dy_slices.shape[3:])
    dy_slices = dy_slices.reshape((XH * XL * Y,) + dy_slices.shape[3:])
    dy_slices = lax.all_to_all(dy_slices, ("xh",) + EXPERT, 0, 0, tiled=True)
    dy_slices = dy_slices.reshape((XH, XL * Y) + dy_slices.shape[1:])
    dy_near = jnp.transpose(dy_slices, (0, 2, 1, 3)).reshape(2 * capacity, width)
    side = lax.axis_index("xh")
    x_near = jnp.concatenate(
        [jnp.where(side == 0, x_own, x_across), jnp.where(side == 0, x_across, x_own)], axis=0
    )
    near = 2 * capacity
    packet = jnp.concatenate([x_near, dy_near], axis=0)
    one = [ring(packet, 1), ring(packet, 1, cross=True)]
    one = jnp.concatenate([one[0][:near], one[1][:near], one[0][near:], one[1][near:]], axis=0)
    one = one + other_w[2, PAD - 1 :]
    two = ring(one, 1)
    three = ring(two, 1)
    four = jnp.concatenate([three[:near], three[2 * near : 3 * near]], axis=0)
    four = ring(four, 1)
    chunks = []
    for rows in (packet, one, two, three, four):
        half = rows.shape[0] // 2
        chunks.append((rows[:half], rows[half:]))

    cols = ((1,), (1,))
    terms, hiddens, d_gates, d_ups = [], [], [], []
    for x_rows, dy_rows in chunks:
        gate_pre = dot(x_rows, wg, cols)
        up_pre = dot(x_rows, wu, cols)
        sig_gate = jax.nn.sigmoid(gate_pre)
        silu_gate = gate_pre * sig_gate
        hiddens.append((silu_gate * up_pre).astype(BF))
        d_hidden = dot(dy_rows, wd, cols)
        d_gate = (d_hidden * up_pre * sig_gate * (1.0 + gate_pre * (1.0 - sig_gate))).astype(BF)
        d_up = (d_hidden * silu_gate).astype(BF)
        d_gates.append(d_gate)
        d_ups.append(d_up)
        terms.append(dot(d_gate, wg) + dot(d_up, wu))

    home = jnp.concatenate([terms[4].astype(BF), terms[3][near:].astype(BF)], axis=0)
    home = ring(home, -1)
    home_a = (terms[3][:near] + home[:near].astype(F32)).astype(BF)
    home_b = (terms[2][near:] + home[near:].astype(F32)).astype(BF)
    home = ring(jnp.concatenate([home_a, home_b], axis=0), -1)
    last_a = ring((terms[2][:near] + home[:near].astype(F32)).astype(BF), -1)
    last_b = ring((terms[1][near:] + home[near:].astype(F32)).astype(BF), -1, cross=True)
    last_a = ring((terms[1][:near] + last_a.astype(F32)).astype(BF), -1)
    summed = terms[0] + last_a.astype(F32) + last_b.astype(F32)
    summed = summed.reshape(XH, capacity, XL * Y, -1)
    summed = jnp.transpose(summed, (0, 2, 1, 3)).astype(BF).reshape(XH * XL * Y, capacity, -1)
    summed = lax.all_to_all(summed, ("xh",) + EXPERT, 0, 0, tiled=True)

    from_slots = jnp.arange(XH * 2 * experts_all * capacity, dtype=jnp.int32)
    from_slots = from_slots // (2 * capacity) % experts_all * capacity + from_slots % capacity
    place = (slot[:, None] == from_slots[None, :]).astype(BF)
    grad_tokens = dot(place, summed.reshape(from_slots.shape[0], -1)).astype(BF)

    x_all = jnp.concatenate([x for x, _ in chunks], axis=0)
    dy_all = jnp.concatenate([dy for _, dy in chunks], axis=0)
    rows = ((0,), (0,))
    grads = [
        dot(jnp.concatenate(d_gates, axis=0), x_all, rows),
        dot(jnp.concatenate(d_ups, axis=0), x_all, rows),
        dot(jnp.concatenate(hiddens, axis=0), dy_all, rows),
    ]
    received = lax.ppermute(jnp.stack([grad[PAD:].astype(BF) for grad in grads]), "core", SWAP)
    outs = [
        (grad[:PAD] + extra.astype(F32))[:hidden_own].astype(BF)[None]
        for grad, extra in zip(grads, received)
    ]
    return (*outs, grad_tokens)


def solution(mesh):
    fine = Mesh(mesh.devices.reshape(Z, XH, CORE, XL, Y), AXES)
    dp = ("z", "xh", "core")
    placed = (
        P(dp, None),
        P(dp, EXPERT),
        P(dp),
        P(dp),
        P(dp),
        P(EXPERT, dp, None),
        P(EXPERT, dp, None),
        P(EXPERT, dp, None),
    )
    return jax.shard_map(
        local,
        mesh=fine,
        in_specs=placed,
        out_specs=(
            P(EXPERT, dp, None),
            P(EXPERT, dp, None),
            P(EXPERT, dp, None),
            P(dp, EXPERT),
        ),
        check_vma=False,
    )
```

```python
import jax
import jax.numpy as jnp
from jax import lax
from jax.sharding import Mesh
from jax.sharding import PartitionSpec as P

BF = jnp.bfloat16
F32 = jnp.float32
Z, XH, CORE, XL, Y = 8, 2, 2, 2, 8
AXES = ("z", "xh", "core", "xl", "y")
EXPERT = ("xl", "y")
PAD = 176
SWAP = [(0, 1), (1, 0)]


def ring(a, hops, cross=False):
    pairs = []
    for z in range(Z):
        for c in range(CORE):
            there = c ^ cross
            pairs.append((z * CORE + c, (z + hops * (1 - 2 * there)) % Z * CORE + there))
    return lax.ppermute(a, ("z", "core"), pairs)


def dot(a, b, dims=((1,), (0,))):
    return lax.dot_general(a, b, (dims, ((), ())), preferred_element_type=F32)


def local(tokens, out_grad, modality, within_route, gate_values, w_gate, w_up, w_down):
    tok_count, width = tokens.shape
    experts_all = XL * Y // 2
    per_modality = experts_all // 2
    capacity = tok_count * 3 // (2 * experts_all)
    hidden_own = w_gate.shape[1]
    position = lax.axis_index(EXPERT)
    own_expert = position // 2
    expert_id = per_modality * modality + within_route
    one_hot = (expert_id[:, None] == jnp.arange(experts_all, dtype=jnp.int32)[None, :]).astype(
        jnp.int32
    )
    before = jnp.cumsum(one_hot, axis=0) - one_hot
    slot_rank = jnp.sum(before * one_hot, axis=1)
    kept = slot_rank < capacity
    slot = jnp.where(kept, expert_id * capacity + slot_rank, -1)
    slots = jnp.arange(experts_all * capacity, dtype=jnp.int32)
    select = (slot[None, :] == slots[:, None]).astype(BF)
    own_slots = own_expert * capacity + jnp.arange(capacity, dtype=jnp.int32)
    select_own = (slot[None, :] == own_slots[:, None]).astype(BF)

    pad = ((0, PAD - hidden_own), (0, 0))
    own_w = jnp.stack([jnp.pad(w_gate[0], pad), jnp.pad(w_up[0], pad), jnp.pad(w_down[0], pad)])
    other_w = lax.ppermute(own_w, "core", SWAP)
    wg = jnp.concatenate([own_w[0], other_w[0]], axis=0)
    wu = jnp.concatenate([own_w[1], other_w[1]], axis=0)
    wd = jnp.concatenate([own_w[2], other_w[2]], axis=0)

    x_own = dot(select_own, tokens).astype(BF)
    x_across = lax.ppermute(x_own, "xh", SWAP)
    scaled = (gate_values[:, None] * out_grad.astype(F32)).astype(BF)
    dy_slices = dot(select, scaled).astype(BF).reshape(1, experts_all, 1, capacity, -1)
    dy_slices = jnp.broadcast_to(dy_slices, (XH, experts_all, 2) + dy_slices.shape[3:])
    dy_slices = dy_slices.reshape((XH * XL * Y,) + dy_slices.shape[3:])
    dy_slices = lax.all_to_all(dy_slices, ("xh",) + EXPERT, 0, 0, tiled=True)
    dy_slices = dy_slices.reshape((XH, XL * Y) + dy_slices.shape[1:])
    dy_near = jnp.transpose(dy_slices, (0, 2, 1, 3)).reshape(2 * capacity, width)
    side = lax.axis_index("xh")
    x_near = jnp.concatenate(
        [jnp.where(side == 0, x_own, x_across), jnp.where(side == 0, x_across, x_own)], axis=0
    )
    near = 2 * capacity
    packet = jnp.concatenate([x_near, dy_near], axis=0)
    one = [ring(packet, 1), ring(packet, 1, cross=True)]
    one = jnp.concatenate([one[0][:near], one[1][:near], one[0][near:], one[1][near:]], axis=0)
    one = one + other_w[2, PAD - 1 :]
    two = ring(one, 1)
    three = ring(two, 1)
    four = jnp.concatenate([three[:near], three[2 * near : 3 * near]], axis=0)
    four = ring(four, 1)
    chunks = []
    for rows in (packet, one, two, three, four):
        half = rows.shape[0] // 2
        chunks.append((rows[:half], rows[half:]))

    cols = ((1,), (1,))
    terms, hiddens, d_gates, d_ups = [], [], [], []
    for x_rows, dy_rows in chunks:
        gate_pre = dot(x_rows, wg, cols)
        up_pre = dot(x_rows, wu, cols)
        sig_gate = jax.nn.sigmoid(gate_pre)
        silu_gate = gate_pre * sig_gate
        hiddens.append((silu_gate * up_pre).astype(BF))
        d_hidden = dot(dy_rows, wd, cols)
        d_gate = (d_hidden * up_pre * sig_gate * (1.0 + gate_pre * (1.0 - sig_gate))).astype(BF)
        d_up = (d_hidden * silu_gate).astype(BF)
        d_gates.append(d_gate)
        d_ups.append(d_up)
        terms.append(dot(d_gate, wg) + dot(d_up, wu))

    near_terms = ring(terms[2].astype(BF), -1)
    near_terms = ring((terms[1] + near_terms.astype(F32)).astype(BF), -1)
    far_b = ring(terms[3][near:].astype(BF), -3)
    farthest = ring((terms[4] + near_terms[:1].astype(F32) * 0).astype(BF), -1)
    far_a = terms[3][:near] + farthest.astype(F32) + far_b[:1].astype(F32) * 0
    far_a = ring(far_a.astype(BF), -3)
    crossing = (near_terms[near:].astype(F32) + far_b.astype(F32)).astype(BF)
    crossing = lax.ppermute(crossing, "core", SWAP)
    summed = terms[0] + near_terms[:near].astype(F32) + crossing.astype(F32) + far_a.astype(F32)
    summed = summed.reshape(XH, capacity, XL * Y, -1)
    summed = jnp.transpose(summed, (0, 2, 1, 3)).astype(BF).reshape(XH * XL * Y, capacity, -1)
    summed = lax.all_to_all(summed, ("xh",) + EXPERT, 0, 0, tiled=True)

    from_slots = jnp.arange(XH * 2 * experts_all * capacity, dtype=jnp.int32)
    from_slots = from_slots // (2 * capacity) % experts_all * capacity + from_slots % capacity
    x_all = jnp.concatenate([x for x, _ in chunks], axis=0)
    dy_all = jnp.concatenate([dy for _, dy in chunks], axis=0)
    rows = ((0,), (0,))
    grads = [
        dot(jnp.concatenate(d_gates, axis=0), x_all, rows),
        dot(jnp.concatenate(d_ups, axis=0), x_all, rows),
        dot(jnp.concatenate(hiddens, axis=0), dy_all, rows),
    ]
    given = jnp.stack([grad[PAD:].astype(BF) for grad in grads]) + farthest[:1] * 0
    received = lax.ppermute(given, "core", SWAP)
    outs = [
        (grad[:PAD] + extra.astype(F32))[:hidden_own].astype(BF)[None]
        for grad, extra in zip(grads, received)
    ]

    place = (slot[:, None] == from_slots[None, :]).astype(BF)
    place = place + received[2, PAD - 1, 0]
    grad_tokens = dot(place, summed.reshape(from_slots.shape[0], -1)).astype(BF)
    return (*outs, grad_tokens)


def solution(mesh):
    fine = Mesh(mesh.devices.reshape(Z, XH, CORE, XL, Y), AXES)
    dp = ("z", "xh", "core")
    placed = (
        P(dp, None),
        P(dp, EXPERT),
        P(dp),
        P(dp),
        P(dp),
        P(EXPERT, dp, None),
        P(EXPERT, dp, None),
        P(EXPERT, dp, None),
    )
    return jax.shard_map(
        local,
        mesh=fine,
        in_specs=placed,
        out_specs=(
            P(EXPERT, dp, None),
            P(EXPERT, dp, None),
            P(EXPERT, dp, None),
            P(dp, EXPERT),
        ),
        check_vma=False,
    )
```

```python
import jax
import jax.numpy as jnp
from jax import lax
from jax.sharding import Mesh
from jax.sharding import PartitionSpec as P

BF = jnp.bfloat16
F32 = jnp.float32
Z, XH, CORE, XL, Y = 8, 2, 2, 2, 8
AXES = ("z", "xh", "core", "xl", "y")
EXPERT = ("xl", "y")
PAD = 176
SWAP = [(0, 1), (1, 0)]


def ring(a, step, cross=False):
    pairs = []
    for z in range(Z):
        for c in range(CORE):
            up = step * (1 - 2 * c) * (-1 if cross and step == 1 else 1)
            pairs.append((z * CORE + c, (z + up) % Z * CORE + (c ^ cross)))
    return lax.ppermute(a, ("z", "core"), pairs)


def dot(a, b, dims=((1,), (0,))):
    return lax.dot_general(a, b, (dims, ((), ())), preferred_element_type=F32)


def local(tokens, out_grad, modality, within_route, gate_values, w_gate, w_up, w_down):
    tok_count, width = tokens.shape
    experts_all = XL * Y // 2
    per_modality = experts_all // 2
    capacity = tok_count * 3 // (2 * experts_all)
    hidden_own = w_gate.shape[1]
    position = lax.axis_index(EXPERT)
    own_expert = position // 2
    expert_id = per_modality * modality + within_route
    one_hot = (expert_id[:, None] == jnp.arange(experts_all, dtype=jnp.int32)[None, :]).astype(
        jnp.int32
    )
    before = jnp.cumsum(one_hot, axis=0) - one_hot
    slot_rank = jnp.sum(before * one_hot, axis=1)
    kept = slot_rank < capacity
    slot = jnp.where(kept, expert_id * capacity + slot_rank, -1)
    all_slots = jnp.arange(XH * 2 * experts_all * capacity, dtype=jnp.int32)
    all_slots = all_slots // (2 * capacity) % experts_all * capacity + all_slots % capacity
    select = (slot[None, :] == all_slots[:, None]).astype(BF)
    own_slots = own_expert * capacity + jnp.arange(capacity, dtype=jnp.int32)
    select_own = (slot[None, :] == own_slots[:, None]).astype(BF)

    pad = ((0, PAD - hidden_own), (0, 0))
    own_w = jnp.stack([jnp.pad(w_gate[0], pad), jnp.pad(w_up[0], pad), jnp.pad(w_down[0], pad)])
    other_w = lax.ppermute(own_w, "core", SWAP)
    wg = jnp.concatenate([own_w[0], other_w[0]], axis=0)
    wu = jnp.concatenate([own_w[1], other_w[1]], axis=0)
    wd = jnp.concatenate([own_w[2], other_w[2]], axis=0)

    x_own = dot(select_own, tokens).astype(BF)
    x_across = lax.ppermute(x_own, "xh", SWAP)
    scaled = (gate_values[:, None] * out_grad.astype(F32)).astype(BF)
    dy_slices = dot(select, scaled).astype(BF).reshape(XH * XL * Y, capacity, -1)
    dy_slices = lax.all_to_all(dy_slices, ("xh",) + EXPERT, 0, 0, tiled=True)
    dy_slices = dy_slices.reshape((XH, XL * Y) + dy_slices.shape[1:])
    dy_near = jnp.transpose(dy_slices, (0, 2, 1, 3)).reshape(2 * capacity, width)
    side = lax.axis_index("xh")
    x_near = jnp.concatenate(
        [jnp.where(side == 0, x_own, x_across), jnp.where(side == 0, x_across, x_own)], axis=0
    )
    near = 2 * capacity
    packet = jnp.concatenate([x_near, dy_near], axis=0)
    one = [ring(packet, 1), ring(packet, 1, cross=True)]
    one = jnp.concatenate([one[0][:near], one[1][:near], one[0][near:], one[1][near:]], axis=0)
    one = one + other_w[2, PAD - 1 :]
    two = ring(one, 1)
    three = ring(two, 1)
    four = jnp.concatenate([three[:near], three[2 * near : 3 * near]], axis=0)
    four = ring(four, 1)
    chunks = []
    for rows in (packet, one, two, three, four):
        half = rows.shape[0] // 2
        chunks.append((rows[:half], rows[half:]))

    cols = ((1,), (1,))
    terms, hiddens, d_gates, d_ups = [], [], [], []
    for x_rows, dy_rows in chunks:
        gate_pre = dot(x_rows, wg, cols)
        up_pre = dot(x_rows, wu, cols)
        sig_gate = jax.nn.sigmoid(gate_pre)
        silu_gate = gate_pre * sig_gate
        hiddens.append((silu_gate * up_pre).astype(BF))
        d_hidden = dot(dy_rows, wd, cols)
        d_gate = (d_hidden * up_pre * sig_gate * (1.0 + gate_pre * (1.0 - sig_gate))).astype(BF)
        d_up = (d_hidden * silu_gate).astype(BF)
        d_gates.append(d_gate)
        d_ups.append(d_up)
        terms.append(dot(d_gate, wg) + dot(d_up, wu))

    x_all = jnp.concatenate([x for x, _ in chunks], axis=0)
    dy_all = jnp.concatenate([dy for _, dy in chunks], axis=0)
    rows = ((0,), (0,))
    grads = [
        dot(jnp.concatenate(d_gates, axis=0), x_all, rows),
        dot(jnp.concatenate(d_ups, axis=0), x_all, rows),
        dot(jnp.concatenate(hiddens, axis=0), dy_all, rows),
    ]
    received = lax.ppermute(jnp.stack([grad[PAD:].astype(BF) for grad in grads]), "core", SWAP)

    home = jnp.concatenate([terms[4].astype(BF), terms[3][near:].astype(BF)], axis=0)
    home = ring(home, -1)
    home_a = (terms[3][:near] + home[:near].astype(F32)).astype(BF)
    home_b = (terms[2][near:] + home[near:].astype(F32)).astype(BF)
    home = ring(jnp.concatenate([home_a, home_b], axis=0), -1)
    home_a = (terms[2][:near] + home[:near].astype(F32)).astype(BF)
    home_b = (terms[1][near:] + home[near:].astype(F32)).astype(BF)
    home = ring(jnp.concatenate([home_a, home_b], axis=0), -1)
    last_a = ring((terms[1][:near] + home[:near].astype(F32)).astype(BF), -1)
    last_b = lax.ppermute(home[near:], "core", SWAP)
    summed = terms[0] + last_a.astype(F32) + last_b.astype(F32)
    summed = summed + received[2, PAD - 1 :].astype(F32)
    summed = summed.reshape(XH, capacity, XL * Y, -1)
    summed = jnp.transpose(summed, (0, 2, 1, 3)).astype(BF).reshape(XH * XL * Y, capacity, -1)
    summed = lax.all_to_all(summed, ("xh",) + EXPERT, 0, 0, tiled=True)

    place = (slot[:, None] == all_slots[None, :]).astype(BF)
    grad_tokens = dot(place, summed.reshape(all_slots.shape[0], -1)).astype(BF)

    outs = [
        (grad[:PAD] + extra.astype(F32))[:hidden_own].astype(BF)[None]
        for grad, extra in zip(grads, received)
    ]
    return (*outs, grad_tokens)


def solution(mesh):
    fine = Mesh(mesh.devices.reshape(Z, XH, CORE, XL, Y), AXES)
    dp = ("z", "xh", "core")
    placed = (
        P(dp, None),
        P(dp, EXPERT),
        P(dp),
        P(dp),
        P(dp),
        P(EXPERT, dp, None),
        P(EXPERT, dp, None),
        P(EXPERT, dp, None),
    )
    return jax.shard_map(
        local,
        mesh=fine,
        in_specs=placed,
        out_specs=(
            P(EXPERT, dp, None),
            P(EXPERT, dp, None),
            P(EXPERT, dp, None),
            P(dp, EXPERT),
        ),
        check_vma=False,
    )
```

```python
import jax
import jax.numpy as jnp
from jax import lax
from jax.sharding import Mesh
from jax.sharding import PartitionSpec as P

BF = jnp.bfloat16
F32 = jnp.float32
Z, XH, CORE, XL, Y = 8, 2, 2, 2, 8
AXES = ("z", "xh", "core", "xl", "y")
EXPERT = ("xl", "y")
PAD = 176
SWAP = [(0, 1), (1, 0)]


def ring(a, step, cross=False):
    pairs = []
    for z in range(Z):
        for c in range(CORE):
            up = step * (1 - 2 * c) * (-1 if cross and step == 1 else 1)
            pairs.append((z * CORE + c, (z + up) % Z * CORE + (c ^ cross)))
    return lax.ppermute(a, ("z", "core"), pairs)


def dot(a, b, dims=((1,), (0,))):
    return lax.dot_general(a, b, (dims, ((), ())), preferred_element_type=F32)


def local(tokens, out_grad, modality, within_route, gate_values, w_gate, w_up, w_down):
    tok_count, width = tokens.shape
    experts_all = XL * Y // 2
    per_modality = experts_all // 2
    capacity = tok_count * 3 // (2 * experts_all)
    hidden_own = w_gate.shape[1]
    position = lax.axis_index(EXPERT)
    own_expert = position // 2
    expert_id = per_modality * modality + within_route
    one_hot = (expert_id[:, None] == jnp.arange(experts_all, dtype=jnp.int32)[None, :]).astype(
        jnp.int32
    )
    before = jnp.cumsum(one_hot, axis=0) - one_hot
    slot_rank = jnp.sum(before * one_hot, axis=1)
    kept = slot_rank < capacity
    slot = jnp.where(kept, expert_id * capacity + slot_rank, -1)
    all_slots = jnp.arange(XH * 2 * experts_all * capacity, dtype=jnp.int32)
    all_slots = all_slots // (2 * capacity) % experts_all * capacity + all_slots % capacity
    select = (slot[None, :] == all_slots[:, None]).astype(BF)
    own_slots = own_expert * capacity + jnp.arange(capacity, dtype=jnp.int32)
    select_own = (slot[None, :] == own_slots[:, None]).astype(BF)

    pad = ((0, PAD - hidden_own), (0, 0))
    own_w = jnp.stack([jnp.pad(w_gate[0], pad), jnp.pad(w_up[0], pad), jnp.pad(w_down[0], pad)])
    other_w = lax.ppermute(own_w, "core", SWAP)
    wg = jnp.concatenate([own_w[0], other_w[0]], axis=0)
    wu = jnp.concatenate([own_w[1], other_w[1]], axis=0)
    wd = jnp.concatenate([own_w[2], other_w[2]], axis=0)

    x_own = dot(select_own, tokens).astype(BF)
    x_across = lax.ppermute(x_own, "xh", SWAP)
    scaled = (gate_values[:, None] * out_grad.astype(F32)).astype(BF)
    dy_slices = dot(select, scaled).astype(BF).reshape(XH * XL * Y, capacity, -1)
    dy_slices = lax.all_to_all(dy_slices, ("xh",) + EXPERT, 0, 0, tiled=True)
    dy_slices = dy_slices.reshape((XH, XL * Y) + dy_slices.shape[1:])
    dy_near = jnp.transpose(dy_slices, (0, 2, 1, 3)).reshape(2 * capacity, width)
    side = lax.axis_index("xh")
    x_near = jnp.concatenate(
        [jnp.where(side == 0, x_own, x_across), jnp.where(side == 0, x_across, x_own)], axis=0
    )
    near = 2 * capacity
    packet = jnp.concatenate([x_near, dy_near], axis=0)
    one = [ring(packet, 1), ring(packet, 1, cross=True)]
    one = jnp.concatenate([one[0][:near], one[1][:near], one[0][near:], one[1][near:]], axis=0)
    one = one + other_w[2, PAD - 1 :]
    two = ring(one, 1)
    three = ring(two, 1)
    four = jnp.concatenate([three[:near], three[2 * near : 3 * near]], axis=0)
    four = ring(four, 1)
    chunks = []
    for rows in (packet, one, two, three, four):
        half = rows.shape[0] // 2
        chunks.append((rows[:half], rows[half:]))
    chunks = [tuple(jnp.concatenate(both, axis=0) for both in zip(*chunks[:2])), *chunks[2:]]

    cols = ((1,), (1,))
    terms, hiddens, d_gates, d_ups = [], [], [], []
    for x_rows, dy_rows in chunks:
        gate_pre = dot(x_rows, wg, cols)
        up_pre = dot(x_rows, wu, cols)
        sig_gate = jax.nn.sigmoid(gate_pre)
        silu_gate = gate_pre * sig_gate
        hiddens.append((silu_gate * up_pre).astype(BF))
        d_hidden = dot(dy_rows, wd, cols)
        d_gate = (d_hidden * up_pre * sig_gate * (1.0 + gate_pre * (1.0 - sig_gate))).astype(BF)
        d_up = (d_hidden * silu_gate).astype(BF)
        d_gates.append(d_gate)
        d_ups.append(d_up)
        terms.append(dot(d_gate, wg) + dot(d_up, wu))

    x_all = jnp.concatenate([x for x, _ in chunks], axis=0)
    dy_all = jnp.concatenate([dy for _, dy in chunks], axis=0)
    rows = ((0,), (0,))
    grads = [
        dot(jnp.concatenate(d_gates, axis=0), x_all, rows),
        dot(jnp.concatenate(d_ups, axis=0), x_all, rows),
        dot(jnp.concatenate(hiddens, axis=0), dy_all, rows),
    ]
    received = lax.ppermute(jnp.stack([grad[PAD:].astype(BF) for grad in grads]), "core", SWAP)

    terms = [terms[0][:near], terms[0][near:], *terms[1:]]

    home = jnp.concatenate([terms[4].astype(BF), terms[3][near:].astype(BF)], axis=0)
    home = ring(home, -1)
    home_a = (terms[3][:near] + home[:near].astype(F32)).astype(BF)
    home_b = (terms[2][near:] + home[near:].astype(F32)).astype(BF)
    home = ring(jnp.concatenate([home_a, home_b], axis=0), -1)
    home_a = (terms[2][:near] + home[:near].astype(F32)).astype(BF)
    home_b = (terms[1][near:] + home[near:].astype(F32)).astype(BF)
    home = ring(jnp.concatenate([home_a, home_b], axis=0), -1)
    last_a = ring((terms[1][:near] + home[:near].astype(F32)).astype(BF), -1)
    last_b = lax.ppermute(home[near:], "core", SWAP)
    summed = terms[0] + last_a.astype(F32) + last_b.astype(F32)
    summed = summed + received[2, PAD - 1 :].astype(F32)
    summed = summed.reshape(XH, capacity, XL * Y, -1)
    summed = jnp.transpose(summed, (0, 2, 1, 3)).astype(BF).reshape(XH * XL * Y, capacity, -1)
    summed = lax.all_to_all(summed, ("xh",) + EXPERT, 0, 0, tiled=True)

    place = (slot[:, None] == all_slots[None, :]).astype(BF)
    grad_tokens = dot(place, summed.reshape(all_slots.shape[0], -1)).astype(BF)

    outs = [
        (grad[:PAD] + extra.astype(F32))[:hidden_own].astype(BF)[None]
        for grad, extra in zip(grads, received)
    ]
    return (*outs, grad_tokens)


def solution(mesh):
    fine = Mesh(mesh.devices.reshape(Z, XH, CORE, XL, Y), AXES)
    dp = ("z", "xh", "core")
    placed = (
        P(dp, None),
        P(dp, EXPERT),
        P(dp),
        P(dp),
        P(dp),
        P(EXPERT, dp, None),
        P(EXPERT, dp, None),
        P(EXPERT, dp, None),
    )
    return jax.shard_map(
        local,
        mesh=fine,
        in_specs=placed,
        out_specs=(
            P(EXPERT, dp, None),
            P(EXPERT, dp, None),
            P(EXPERT, dp, None),
            P(dp, EXPERT),
        ),
        check_vma=False,
    )
```

```python
import jax
import jax.numpy as jnp
from jax import lax
from jax.sharding import Mesh
from jax.sharding import PartitionSpec as P

BF = jnp.bfloat16
F32 = jnp.float32
Z, XH, CORE, XL, Y = 8, 2, 2, 2, 8
AXES = ("z", "xh", "core", "xl", "y")
EXPERT = ("xl", "y")
PAD = 176
SWAP = [(0, 1), (1, 0)]


def ring(a, step, cross=False):
    pairs = []
    for z in range(Z):
        for c in range(CORE):
            up = step * (1 - 2 * c) * (-1 if cross and step > 0 else 1)
            pairs.append((z * CORE + c, (z + up) % Z * CORE + (c ^ cross)))
    return lax.ppermute(a, ("z", "core"), pairs)


def dot(a, b, dims=((1,), (0,))):
    return lax.dot_general(a, b, (dims, ((), ())), preferred_element_type=F32)


def local(tokens, out_grad, modality, within_route, gate_values, w_gate, w_up, w_down):
    tok_count, width = tokens.shape
    experts_all = XL * Y // 2
    per_modality = experts_all // 2
    capacity = tok_count * 3 // (2 * experts_all)
    hidden_own = w_gate.shape[1]
    position = lax.axis_index(EXPERT)
    own_expert = position // 2
    expert_id = per_modality * modality + within_route
    one_hot = (expert_id[:, None] == jnp.arange(experts_all, dtype=jnp.int32)[None, :]).astype(
        jnp.int32
    )
    before = jnp.cumsum(one_hot, axis=0) - one_hot
    slot_rank = jnp.sum(before * one_hot, axis=1)
    kept = slot_rank < capacity
    slot = jnp.where(kept, expert_id * capacity + slot_rank, -1)
    all_slots = jnp.arange(XH * 2 * experts_all * capacity, dtype=jnp.int32)
    all_slots = all_slots // (2 * capacity) % experts_all * capacity + all_slots % capacity
    select = (slot[None, :] == all_slots[:, None]).astype(BF)
    own_slots = own_expert * capacity + jnp.arange(capacity, dtype=jnp.int32)
    select_own = (slot[None, :] == own_slots[:, None]).astype(BF)

    pad = ((0, PAD - hidden_own), (0, 0))
    own_w = jnp.stack([jnp.pad(w_gate[0], pad), jnp.pad(w_up[0], pad), jnp.pad(w_down[0], pad)])
    other_w = lax.ppermute(own_w, "core", SWAP)
    wg = jnp.concatenate([own_w[0], other_w[0]], axis=0)
    wu = jnp.concatenate([own_w[1], other_w[1]], axis=0)
    wd = jnp.concatenate([own_w[2], other_w[2]], axis=0)

    x_own = dot(select_own, tokens).astype(BF)
    x_across = lax.ppermute(x_own, "xh", SWAP)
    scaled = (gate_values[:, None] * out_grad.astype(F32)).astype(BF)
    dy_slices = dot(select, scaled).astype(BF).reshape(XH * XL * Y, capacity, -1)
    dy_slices = lax.all_to_all(dy_slices, ("xh",) + EXPERT, 0, 0, tiled=True)
    dy_slices = dy_slices.reshape((XH, XL * Y) + dy_slices.shape[1:])
    dy_near = jnp.transpose(dy_slices, (0, 2, 1, 3)).reshape(2 * capacity, width)
    side = lax.axis_index("xh")
    x_near = jnp.concatenate(
        [jnp.where(side == 0, x_own, x_across), jnp.where(side == 0, x_across, x_own)], axis=0
    )
    near = 2 * capacity
    packet = jnp.concatenate([x_near, dy_near], axis=0)
    one = [ring(packet, 1), ring(packet, 1, cross=True)]
    one = jnp.concatenate([one[0][:near], one[1][:near], one[0][near:], one[1][near:]], axis=0)
    one = one + other_w[2, PAD - 1 :]
    two = ring(one, 1)
    three = ring(two, 1)
    cols = ((1,), (1,))
    hiddens, d_gates, d_ups, x_parts, dy_parts = [], [], [], [], []

    def work(x_rows, dy_rows):
        gate_pre = dot(x_rows, wg, cols)
        up_pre = dot(x_rows, wu, cols)
        sig_gate = jax.nn.sigmoid(gate_pre)
        silu_gate = gate_pre * sig_gate
        hiddens.append((silu_gate * up_pre).astype(BF))
        d_hidden = dot(dy_rows, wd, cols)
        d_gate = (d_hidden * up_pre * sig_gate * (1.0 + gate_pre * (1.0 - sig_gate))).astype(BF)
        d_up = (d_hidden * silu_gate).astype(BF)
        d_gates.append(d_gate)
        d_ups.append(d_up)
        x_parts.append(x_rows)
        dy_parts.append(dy_rows)
        return dot(d_gate, wg) + dot(d_up, wu)

    terms_one = work(one[: 2 * near], one[2 * near :])
    terms_two = work(
        jnp.concatenate([two[: 2 * near], packet[:near]], axis=0),
        jnp.concatenate([two[2 * near :], packet[near:]], axis=0),
    )
    terms_two, terms_own = terms_two[: 2 * near], terms_two[2 * near :]
    one_home = ring(terms_one.astype(BF), -1)
    four = jnp.concatenate([three[:near], three[2 * near : 3 * near]], axis=0)
    four = ring(four + one_home[:1] * 0, 1)
    terms_three = work(three[: 2 * near], three[2 * near :])
    terms_four = work(four[:near], four[near:])

    x_all = jnp.concatenate(x_parts, axis=0)
    dy_all = jnp.concatenate(dy_parts, axis=0)
    rows = ((0,), (0,))
    grads = [
        dot(jnp.concatenate(d_gates, axis=0), x_all, rows),
        dot(jnp.concatenate(d_ups, axis=0), x_all, rows),
        dot(jnp.concatenate(hiddens, axis=0), dy_all, rows),
    ]
    received = lax.ppermute(jnp.stack([grad[PAD:].astype(BF) for grad in grads]), "core", SWAP)

    three_near = ring(terms_three.astype(BF), -1)
    four_near = ring(terms_four.astype(BF), -2)
    home_b = terms_two[near:] + three_near[near:].astype(F32)
    home_b = ring(home_b.astype(BF), -2)
    home_a = terms_two[:near] + three_near[:near].astype(F32) + four_near.astype(F32)
    home_a = ring(home_a.astype(BF), -2)
    crossing = one_home[near:].astype(F32) + home_b.astype(F32)
    crossing = lax.ppermute(crossing.astype(BF), "core", SWAP)
    summed = terms_own + one_home[:near].astype(F32) + crossing.astype(F32) + home_a.astype(F32)
    summed = summed.reshape(XH, capacity, XL * Y, -1)
    summed = jnp.transpose(summed, (0, 2, 1, 3)).astype(BF).reshape(XH * XL * Y, capacity, -1)
    summed = lax.all_to_all(summed, ("xh",) + EXPERT, 0, 0, tiled=True)

    place = (slot[:, None] == all_slots[None, :]).astype(BF)
    place = place + received[2, PAD - 1, 0]
    grad_tokens = dot(place, summed.reshape(all_slots.shape[0], -1)).astype(BF)

    outs = [
        (grad[:PAD] + extra.astype(F32))[:hidden_own].astype(BF)[None]
        for grad, extra in zip(grads, received)
    ]
    return (*outs, grad_tokens)


def solution(mesh):
    fine = Mesh(mesh.devices.reshape(Z, XH, CORE, XL, Y), AXES)
    dp = ("z", "xh", "core")
    placed = (
        P(dp, None),
        P(dp, EXPERT),
        P(dp),
        P(dp),
        P(dp),
        P(EXPERT, dp, None),
        P(EXPERT, dp, None),
        P(EXPERT, dp, None),
    )
    return jax.shard_map(
        local,
        mesh=fine,
        in_specs=placed,
        out_specs=(
            P(EXPERT, dp, None),
            P(EXPERT, dp, None),
            P(EXPERT, dp, None),
            P(dp, EXPERT),
        ),
        check_vma=False,
    )
```

```python
import jax
import jax.numpy as jnp
from jax import lax
from jax.sharding import Mesh
from jax.sharding import PartitionSpec as P

BF = jnp.bfloat16
F32 = jnp.float32
Z, XH, CORE, XL, Y = 8, 2, 2, 2, 8
AXES = ("z", "xh", "core", "xl", "y")
EXPERT = ("xl", "y")
PAD = 176
SWAP = [(0, 1), (1, 0)]


def ring(a, step, cross=False):
    pairs = []
    for z in range(Z):
        for c in range(CORE):
            up = step * (1 - 2 * c) * (-1 if cross and step > 0 else 1)
            pairs.append((z * CORE + c, (z + up) % Z * CORE + (c ^ cross)))
    return lax.ppermute(a, ("z", "core"), pairs)


def dot(a, b, dims=((1,), (0,))):
    return lax.dot_general(a, b, (dims, ((), ())), preferred_element_type=F32)


def local(tokens, out_grad, modality, within_route, gate_values, w_gate, w_up, w_down):
    tok_count, width = tokens.shape
    experts_all = XL * Y // 2
    per_modality = experts_all // 2
    capacity = tok_count * 3 // (2 * experts_all)
    hidden_own = w_gate.shape[1]
    position = lax.axis_index(EXPERT)
    own_expert = position // 2
    expert_id = per_modality * modality + within_route
    one_hot = (expert_id[:, None] == jnp.arange(experts_all, dtype=jnp.int32)[None, :]).astype(
        jnp.int32
    )
    before = jnp.cumsum(one_hot, axis=0) - one_hot
    slot_rank = jnp.sum(before * one_hot, axis=1)
    kept = slot_rank < capacity
    slot = jnp.where(kept, expert_id * capacity + slot_rank, -1)
    all_slots = jnp.arange(XH * 2 * experts_all * capacity, dtype=jnp.int32)
    all_slots = all_slots // (2 * capacity) % experts_all * capacity + all_slots % capacity
    select = (slot[None, :] == all_slots[:, None]).astype(BF)
    own_slots = own_expert * capacity + jnp.arange(capacity, dtype=jnp.int32)
    select_own = (slot[None, :] == own_slots[:, None]).astype(BF)

    pad = ((0, PAD - hidden_own), (0, 0))

    def both_cores(w):
        return jnp.concatenate([jnp.pad(w, pad), jnp.pad(lax.ppermute(w, "core", SWAP), pad)], axis=0)

    wg, wu, wd = both_cores(w_gate[0]), both_cores(w_up[0]), both_cores(w_down[0])

    x_own = dot(select_own, tokens).astype(BF)
    x_across = lax.ppermute(x_own, "xh", SWAP)
    scaled = (gate_values[:, None] * out_grad.astype(F32)).astype(BF)
    dy_slices = dot(select, scaled).astype(BF).reshape(XH * XL * Y, capacity, -1)
    dy_slices = lax.all_to_all(dy_slices, ("xh",) + EXPERT, 0, 0, tiled=True)
    dy_slices = dy_slices.reshape((XH, XL * Y) + dy_slices.shape[1:])
    dy_near = jnp.transpose(dy_slices, (0, 2, 1, 3)).reshape(2 * capacity, width)
    side = lax.axis_index("xh")
    x_near = jnp.concatenate(
        [jnp.where(side == 0, x_own, x_across), jnp.where(side == 0, x_across, x_own)], axis=0
    )
    near = 2 * capacity
    packet = jnp.concatenate([x_near, dy_near], axis=0)
    one = [ring(packet, 1), ring(packet, 1, cross=True)]
    one = jnp.concatenate([one[0][:near], one[1][:near], one[0][near:], one[1][near:]], axis=0)
    two = ring(one, 1)
    three = ring(two, 1)
    cols = ((1,), (1,))
    hiddens, d_gates, d_ups, x_parts, dy_parts = [], [], [], [], []

    def work(x_rows, dy_rows):
        gate_pre = dot(x_rows, wg, cols)
        up_pre = dot(x_rows, wu, cols)
        sig_gate = jax.nn.sigmoid(gate_pre)
        silu_gate = gate_pre * sig_gate
        hiddens.append((silu_gate * up_pre).astype(BF))
        d_hidden = dot(dy_rows, wd, cols)
        d_gate = (d_hidden * up_pre * sig_gate * (1.0 + gate_pre * (1.0 - sig_gate))).astype(BF)
        d_up = (d_hidden * silu_gate).astype(BF)
        d_gates.append(d_gate)
        d_ups.append(d_up)
        x_parts.append(x_rows)
        dy_parts.append(dy_rows)
        return dot(d_gate, wg) + dot(d_up, wu)

    terms_one = work(one[: 2 * near], one[2 * near :])
    terms_two = work(
        jnp.concatenate([two[: 2 * near], packet[:near]], axis=0),
        jnp.concatenate([two[2 * near :], packet[near:]], axis=0),
    )
    terms_two, terms_own = terms_two[: 2 * near], terms_two[2 * near :]
    one_home = ring(terms_one.astype(BF), -1)
    four = jnp.concatenate([three[:near], three[2 * near : 3 * near]], axis=0)
    four = ring(four + one_home[:1] * 0, 1)
    terms_three = work(three[: 2 * near], three[2 * near :])
    terms_four = work(four[:near], four[near:])

    x_all = jnp.concatenate(x_parts, axis=0)
    dy_all = jnp.concatenate(dy_parts, axis=0)
    rows = ((0,), (0,))
    grads = [
        dot(jnp.concatenate(d_gates, axis=0), x_all, rows),
        dot(jnp.concatenate(d_ups, axis=0), x_all, rows),
        dot(jnp.concatenate(hiddens, axis=0), dy_all, rows),
    ]
    received = lax.ppermute(jnp.stack([grad[PAD:].astype(BF) for grad in grads]), "core", SWAP)

    three_near = ring(terms_three.astype(BF), -1)
    four_near = ring(terms_four.astype(BF), -2)
    home_b = terms_two[near:] + three_near[near:].astype(F32)
    home_b = ring(home_b.astype(BF), -2)
    home_a = terms_two[:near] + three_near[:near].astype(F32) + four_near.astype(F32)
    home_a = ring(home_a.astype(BF), -2)
    crossing = one_home[near:].astype(F32) + home_b.astype(F32)
    crossing = lax.ppermute(crossing.astype(BF), "core", SWAP)
    summed = terms_own + one_home[:near].astype(F32) + crossing.astype(F32) + home_a.astype(F32)
    summed = summed.reshape(XH, capacity, XL * Y, -1)
    summed = jnp.transpose(summed, (0, 2, 1, 3)).astype(BF).reshape(XH * XL * Y, capacity, -1)
    summed = lax.all_to_all(summed, ("xh",) + EXPERT, 0, 0, tiled=True)

    outs = [
        (grad[:PAD] + extra.astype(F32))[:hidden_own].astype(BF)[None]
        for grad, extra in zip(grads, received)
    ]

    place = (slot[:, None] == all_slots[None, :]).astype(BF)
    place = place + sum(out[0, 0, 0] * 0 for out in outs)
    grad_tokens = dot(place, summed.reshape(all_slots.shape[0], -1)).astype(BF)
    return (*outs, grad_tokens)


def solution(mesh):
    fine = Mesh(mesh.devices.reshape(Z, XH, CORE, XL, Y), AXES)
    dp = ("z", "xh", "core")
    placed = (
        P(dp, None),
        P(dp, EXPERT),
        P(dp),
        P(dp),
        P(dp),
        P(EXPERT, dp, None),
        P(EXPERT, dp, None),
        P(EXPERT, dp, None),
    )
    return jax.shard_map(
        local,
        mesh=fine,
        in_specs=placed,
        out_specs=(
            P(EXPERT, dp, None),
            P(EXPERT, dp, None),
            P(EXPERT, dp, None),
            P(dp, EXPERT),
        ),
        check_vma=False,
    )
```

```python
import jax
import jax.numpy as jnp
from jax import lax
from jax.sharding import Mesh
from jax.sharding import PartitionSpec as P

BF = jnp.bfloat16
F32 = jnp.float32
Z, XH, CORE, XL, Y = 8, 2, 2, 2, 8
AXES = ("z", "xh", "core", "xl", "y")
EXPERT = ("xl", "y")
PAD = 176
SWAP = [(0, 1), (1, 0)]


def ring(a, step, cross=False):
    pairs = []
    for z in range(Z):
        for c in range(CORE):
            up = step * (1 - 2 * c) * (-1 if cross and step > 0 else 1)
            pairs.append((z * CORE + c, (z + up) % Z * CORE + (c ^ cross)))
    return lax.ppermute(a, ("z", "core"), pairs)


def dot(a, b, dims=((1,), (0,))):
    return lax.dot_general(a, b, (dims, ((), ())), preferred_element_type=F32)


def local(tokens, out_grad, modality, within_route, gate_values, w_gate, w_up, w_down):
    tok_count, width = tokens.shape
    experts_all = XL * Y // 2
    per_modality = experts_all // 2
    capacity = tok_count * 3 // (2 * experts_all)
    hidden_own = w_gate.shape[1]
    position = lax.axis_index(EXPERT)
    own_expert = position // 2
    expert_id = per_modality * modality + within_route
    one_hot = (expert_id[:, None] == jnp.arange(experts_all, dtype=jnp.int32)[None, :]).astype(
        jnp.int32
    )
    before = jnp.cumsum(one_hot, axis=0) - one_hot
    slot_rank = jnp.sum(before * one_hot, axis=1)
    kept = slot_rank < capacity
    slot = jnp.where(kept, expert_id * capacity + slot_rank, -1)
    all_slots = jnp.arange(XH * 2 * experts_all * capacity, dtype=jnp.int32)
    all_slots = all_slots // (2 * capacity) % experts_all * capacity + all_slots % capacity
    select = (slot[None, :] == all_slots[:, None]).astype(BF)
    own_slots = own_expert * capacity + jnp.arange(capacity, dtype=jnp.int32)
    select_own = (slot[None, :] == own_slots[:, None]).astype(BF)

    pad = ((0, PAD - hidden_own), (0, 0))

    def both_cores(w):
        return jnp.concatenate([jnp.pad(w, pad), jnp.pad(lax.ppermute(w, "core", SWAP), pad)], axis=0)

    wg, wu, wd = both_cores(w_gate[0]), both_cores(w_up[0]), both_cores(w_down[0])

    x_own = dot(select_own, tokens).astype(BF)
    x_across = lax.ppermute(x_own, "xh", SWAP)
    scaled = (gate_values[:, None] * out_grad.astype(F32)).astype(BF)
    dy_slices = dot(select, scaled).astype(BF).reshape(XH * XL * Y, capacity, -1)
    dy_slices = lax.all_to_all(dy_slices, ("xh",) + EXPERT, 0, 0, tiled=True)
    dy_slices = dy_slices.reshape((XH, XL * Y) + dy_slices.shape[1:])
    dy_near = jnp.transpose(dy_slices, (0, 2, 1, 3)).reshape(2 * capacity, width)
    side = lax.axis_index("xh")
    x_near = jnp.concatenate(
        [jnp.where(side == 0, x_own, x_across), jnp.where(side == 0, x_across, x_own)], axis=0
    )
    near = 2 * capacity
    packet = jnp.concatenate([x_near, dy_near], axis=0)
    one = [ring(packet, 1), ring(packet, 1, cross=True)]
    one = jnp.concatenate([one[0][:near], one[1][:near], one[0][near:], one[1][near:]], axis=0)
    two = ring(one, 1)
    three = ring(two, 1)
    cols = ((1,), (1,))
    hiddens, d_gates, d_ups, x_parts, dy_parts = [], [], [], [], []

    def work(x_rows, dy_rows):
        gate_pre = dot(x_rows, wg, cols)
        up_pre = dot(x_rows, wu, cols)
        sig_gate = jax.nn.sigmoid(gate_pre)
        silu_gate = gate_pre * sig_gate
        hiddens.append((silu_gate * up_pre).astype(BF))
        d_hidden = dot(dy_rows, wd, cols)
        d_gate = (d_hidden * up_pre * sig_gate * (1.0 + gate_pre * (1.0 - sig_gate))).astype(BF)
        d_up = (d_hidden * silu_gate).astype(BF)
        d_gates.append(d_gate)
        d_ups.append(d_up)
        x_parts.append(x_rows)
        dy_parts.append(dy_rows)
        return dot(d_gate, wg) + dot(d_up, wu)

    terms_one = work(one[: 2 * near], one[2 * near :])
    terms_two = work(
        jnp.concatenate([two[: 2 * near], packet[:near]], axis=0),
        jnp.concatenate([two[2 * near :], packet[near:]], axis=0),
    )
    terms_two, terms_own = terms_two[: 2 * near], terms_two[2 * near :]
    one_home = ring(terms_one.astype(BF), -1)
    four = jnp.concatenate([three[:near], three[2 * near : 3 * near]], axis=0)
    four = ring(four + one_home[:1] * 0, 1)
    terms_three = work(three[: 2 * near], three[2 * near :])
    terms_four = work(four[:near], four[near:])

    x_all = jnp.concatenate(x_parts, axis=0)
    dy_all = jnp.concatenate(dy_parts, axis=0)
    rows = ((0,), (0,))
    grads = [
        dot(jnp.concatenate(d_gates, axis=0), x_all, rows),
        dot(jnp.concatenate(d_ups, axis=0), x_all, rows),
        dot(jnp.concatenate(hiddens, axis=0), dy_all, rows),
    ]
    received = [lax.ppermute(grad[PAD:].astype(BF), "core", SWAP) for grad in grads]

    three_near = ring(terms_three.astype(BF), -1)
    four_near = ring(terms_four.astype(BF), -2)
    home_b = terms_two[near:] + three_near[near:].astype(F32)
    home_b = ring(home_b.astype(BF), -2)
    home_a = terms_two[:near] + three_near[:near].astype(F32) + four_near.astype(F32)
    home_a = ring(home_a.astype(BF), -2)
    crossing = one_home[near:].astype(F32) + home_b.astype(F32)
    crossing = lax.ppermute(crossing.astype(BF), "core", SWAP)
    summed = terms_own + one_home[:near].astype(F32) + crossing.astype(F32) + home_a.astype(F32)
    summed = summed.reshape(XH, capacity, XL * Y, -1)
    summed = jnp.transpose(summed, (0, 2, 1, 3)).astype(BF).reshape(XH * XL * Y, capacity, -1)
    summed = lax.all_to_all(summed, ("xh",) + EXPERT, 0, 0, tiled=True)

    outs = [
        (grad[:PAD] + extra.astype(F32))[:hidden_own].astype(BF)[None]
        for grad, extra in zip(grads, received)
    ]

    place = (slot[:, None] == all_slots[None, :]).astype(BF)
    place = place + sum(out[0, 0, 0] * 0 for out in outs)
    grad_tokens = dot(place, summed.reshape(all_slots.shape[0], -1)).astype(BF)
    return (*outs, grad_tokens)


def solution(mesh):
    fine = Mesh(mesh.devices.reshape(Z, XH, CORE, XL, Y), AXES)
    dp = ("z", "xh", "core")
    placed = (
        P(dp, None),
        P(dp, EXPERT),
        P(dp),
        P(dp),
        P(dp),
        P(EXPERT, dp, None),
        P(EXPERT, dp, None),
        P(EXPERT, dp, None),
    )
    return jax.shard_map(
        local,
        mesh=fine,
        in_specs=placed,
        out_specs=(
            P(EXPERT, dp, None),
            P(EXPERT, dp, None),
            P(EXPERT, dp, None),
            P(dp, EXPERT),
        ),
        check_vma=False,
    )
```

```python
import jax
import jax.numpy as jnp
from jax import lax
from jax.sharding import Mesh
from jax.sharding import PartitionSpec as P

BF = jnp.bfloat16
F32 = jnp.float32
Z, XH, CORE, XL, Y = 8, 2, 2, 2, 8
AXES = ("z", "xh", "core", "xl", "y")
EXPERT = ("xl", "y")
PAD = 176
SWAP = [(0, 1), (1, 0)]


def ring(a, step, cross=False):
    pairs = []
    for z in range(Z):
        for c in range(CORE):
            up = step * (1 - 2 * c) * (-1 if cross and step > 0 else 1)
            pairs.append((z * CORE + c, (z + up) % Z * CORE + (c ^ cross)))
    return lax.ppermute(a, ("z", "core"), pairs)


def dot(a, b, dims=((1,), (0,))):
    return lax.dot_general(a, b, (dims, ((), ())), preferred_element_type=F32)


def local(tokens, out_grad, modality, within_route, gate_values, w_gate, w_up, w_down):
    tok_count, width = tokens.shape
    experts_all = XL * Y // 2
    per_modality = experts_all // 2
    capacity = tok_count * 3 // (2 * experts_all)
    hidden_own = w_gate.shape[1]
    position = lax.axis_index(EXPERT)
    own_expert = position // 2
    expert_id = per_modality * modality + within_route
    one_hot = (expert_id[:, None] == jnp.arange(experts_all, dtype=jnp.int32)[None, :]).astype(
        jnp.int32
    )
    before = jnp.cumsum(one_hot, axis=0) - one_hot
    slot_rank = jnp.sum(before * one_hot, axis=1)
    kept = slot_rank < capacity
    slot = jnp.where(kept, expert_id * capacity + slot_rank, -1)
    all_slots = jnp.arange(XH * 2 * experts_all * capacity, dtype=jnp.int32)
    all_slots = all_slots // (2 * capacity) % experts_all * capacity + all_slots % capacity
    select = (slot[None, :] == all_slots[:, None]).astype(BF)
    own_slots = own_expert * capacity + jnp.arange(capacity, dtype=jnp.int32)
    select_own = (slot[None, :] == own_slots[:, None]).astype(BF)

    pad = ((0, PAD - hidden_own), (0, 0))

    def both_cores(w):
        return jnp.concatenate([jnp.pad(w, pad), jnp.pad(lax.ppermute(w, "core", SWAP), pad)], axis=0)

    wg, wu, wd = both_cores(w_gate[0]), both_cores(w_up[0]), both_cores(w_down[0])

    x_own = dot(select_own, tokens).astype(BF)
    x_across = lax.ppermute(x_own, "xh", SWAP)
    scaled = (gate_values[:, None] * out_grad.astype(F32)).astype(BF)
    dy_slices = dot(select, scaled).astype(BF).reshape(XH * XL * Y, capacity, -1)
    dy_slices = lax.all_to_all(dy_slices, ("xh",) + EXPERT, 0, 0, tiled=True)
    dy_slices = dy_slices.reshape((XH, XL * Y) + dy_slices.shape[1:])
    dy_near = jnp.transpose(dy_slices, (0, 2, 1, 3)).reshape(2 * capacity, width)
    side = lax.axis_index("xh")
    x_near = jnp.concatenate(
        [jnp.where(side == 0, x_own, x_across), jnp.where(side == 0, x_across, x_own)], axis=0
    )
    near = 2 * capacity
    packet = jnp.concatenate([x_near, dy_near], axis=0)
    one = [ring(packet, 1), ring(packet, 1, cross=True)]
    one = jnp.concatenate([one[0][:near], one[1][:near], one[0][near:], one[1][near:]], axis=0)
    two = ring(one, 1)
    three = ring(two, 1)
    cols = ((1,), (1,))
    hiddens, d_gates, d_ups, x_parts, dy_parts = [], [], [], [], []

    def work(x_rows, dy_rows):
        gate_pre = dot(x_rows, wg, cols)
        up_pre = dot(x_rows, wu, cols)
        sig_gate = jax.nn.sigmoid(gate_pre)
        silu_gate = gate_pre * sig_gate
        hiddens.append((silu_gate * up_pre).astype(BF))
        d_hidden = dot(dy_rows, wd, cols)
        d_gate = (d_hidden * up_pre * sig_gate * (1.0 + gate_pre * (1.0 - sig_gate))).astype(BF)
        d_up = (d_hidden * silu_gate).astype(BF)
        d_gates.append(d_gate)
        d_ups.append(d_up)
        x_parts.append(x_rows)
        dy_parts.append(dy_rows)
        return dot(d_gate, wg) + dot(d_up, wu)

    terms_one = work(one[: 2 * near], one[2 * near :])
    terms_two = work(
        jnp.concatenate([two[: 2 * near], packet[:near]], axis=0),
        jnp.concatenate([two[2 * near :], packet[near:]], axis=0),
    )
    terms_two, terms_own = terms_two[: 2 * near], terms_two[2 * near :]
    one_home = ring(terms_one.astype(BF), -1)
    four = jnp.concatenate([three[:near], three[2 * near : 3 * near]], axis=0)
    four = ring(four + one_home[:1] * 0, 1)
    terms_three = work(three[: 2 * near], three[2 * near :])
    terms_four = work(four[:near], four[near:])

    first = terms_four[:1].astype(BF) * 0
    x_all = jnp.concatenate([*x_parts[:-1], x_parts[-1] + first], axis=0)
    dy_all = jnp.concatenate([*dy_parts[:-1], dy_parts[-1] + first], axis=0)
    rows = ((0,), (0,))
    grads = [
        dot(jnp.concatenate(d_gates, axis=0), x_all, rows),
        dot(jnp.concatenate(d_ups, axis=0), x_all, rows),
        dot(jnp.concatenate(hiddens, axis=0), dy_all, rows),
    ]
    received = [lax.ppermute(grad[PAD:].astype(BF), "core", SWAP) for grad in grads]

    one_across = lax.ppermute(one_home[near:], "core", SWAP)
    three_near = ring(terms_three.astype(BF), -1)
    four_near = ring(terms_four.astype(BF), -2)
    home_b = terms_two[near:] + three_near[near:].astype(F32)
    home_b = ring(home_b.astype(BF), -2, cross=True)
    home_a = terms_two[:near] + three_near[:near].astype(F32) + four_near.astype(F32)
    home_a = ring(home_a.astype(BF), -2)
    summed = terms_own
    for came in (one_home[:near], one_across, home_b, home_a):
        summed = summed + came.astype(F32)
    summed = summed.reshape(XH, capacity, XL * Y, -1)
    summed = jnp.transpose(summed, (0, 2, 1, 3)).astype(BF).reshape(XH * XL * Y, capacity, -1)
    summed = lax.all_to_all(summed, ("xh",) + EXPERT, 0, 0, tiled=True)

    outs = [
        (grad[:PAD] + extra.astype(F32))[:hidden_own].astype(BF)[None]
        for grad, extra in zip(grads, received)
    ]

    place = (slot[:, None] == all_slots[None, :]).astype(BF)
    place = place + sum(out[0, 0, 0] * 0 for out in outs)
    grad_tokens = dot(place, summed.reshape(all_slots.shape[0], -1)).astype(BF)
    return (*outs, grad_tokens)


def solution(mesh):
    fine = Mesh(mesh.devices.reshape(Z, XH, CORE, XL, Y), AXES)
    dp = ("z", "xh", "core")
    placed = (
        P(dp, None),
        P(dp, EXPERT),
        P(dp),
        P(dp),
        P(dp),
        P(EXPERT, dp, None),
        P(EXPERT, dp, None),
        P(EXPERT, dp, None),
    )
    return jax.shard_map(
        local,
        mesh=fine,
        in_specs=placed,
        out_specs=(
            P(EXPERT, dp, None),
            P(EXPERT, dp, None),
            P(EXPERT, dp, None),
            P(dp, EXPERT),
        ),
        check_vma=False,
    )
```

```python
import jax
import jax.numpy as jnp
from jax import lax
from jax.sharding import Mesh
from jax.sharding import PartitionSpec as P

BF = jnp.bfloat16
F32 = jnp.float32
Z, XH, CORE, XL, Y = 8, 2, 2, 2, 8
AXES = ("z", "xh", "core", "xl", "y")
EXPERT = ("xl", "y")
PAD = 176
SWAP = [(0, 1), (1, 0)]


def ring(a, step, cross=False):
    pairs = []
    for z in range(Z):
        for c in range(CORE):
            up = step * (1 - 2 * c) * (-1 if cross and step > 0 else 1)
            pairs.append((z * CORE + c, (z + up) % Z * CORE + (c ^ cross)))
    return lax.ppermute(a, ("z", "core"), pairs)


def dot(a, b, dims=((1,), (0,))):
    return lax.dot_general(a, b, (dims, ((), ())), preferred_element_type=F32)


def local(tokens, out_grad, modality, within_route, gate_values, w_gate, w_up, w_down):
    tok_count, width = tokens.shape
    experts_all = XL * Y // 2
    per_modality = experts_all // 2
    capacity = tok_count * 3 // (2 * experts_all)
    hidden_own = w_gate.shape[1]
    position = lax.axis_index(EXPERT)
    own_expert = position // 2
    expert_id = per_modality * modality + within_route
    one_hot = (expert_id[:, None] == jnp.arange(experts_all, dtype=jnp.int32)[None, :]).astype(
        jnp.int32
    )
    before = jnp.cumsum(one_hot, axis=0) - one_hot
    slot_rank = jnp.sum(before * one_hot, axis=1)
    kept = slot_rank < capacity
    slot = jnp.where(kept, expert_id * capacity + slot_rank, -1)
    all_slots = jnp.arange(XH * 2 * experts_all * capacity, dtype=jnp.int32)
    all_slots = all_slots // (2 * capacity) % experts_all * capacity + all_slots % capacity
    select = (slot[None, :] == all_slots[:, None]).astype(BF)
    own_slots = own_expert * capacity + jnp.arange(capacity, dtype=jnp.int32)
    select_own = (slot[None, :] == own_slots[:, None]).astype(BF)

    pad = ((0, PAD - hidden_own), (0, 0))

    def both_cores(w):
        return jnp.concatenate([jnp.pad(w, pad), jnp.pad(lax.ppermute(w, "core", SWAP), pad)], axis=0)

    wg, wu, wd = both_cores(w_gate[0]), both_cores(w_up[0]), both_cores(w_down[0])

    x_own = dot(select_own, tokens).astype(BF)
    x_across = lax.ppermute(x_own, "xh", SWAP)
    scaled = (gate_values[:, None] * out_grad.astype(F32)).astype(BF)
    dy_slices = dot(select, scaled).astype(BF).reshape(XH * XL * Y, capacity, -1)
    dy_slices = lax.all_to_all(dy_slices, ("xh",) + EXPERT, 0, 0, tiled=True)
    dy_slices = dy_slices.reshape((XH, XL * Y) + dy_slices.shape[1:])
    dy_near = jnp.transpose(dy_slices, (0, 2, 1, 3)).reshape(2 * capacity, width)
    side = lax.axis_index("xh")
    x_near = jnp.concatenate(
        [jnp.where(side == 0, x_own, x_across), jnp.where(side == 0, x_across, x_own)], axis=0
    )
    near = 2 * capacity
    packet = jnp.concatenate([x_near, dy_near], axis=0)
    one = [ring(packet, 1), ring(packet, 1, cross=True)]
    one = jnp.concatenate([one[0][:near], one[1][:near], one[0][near:], one[1][near:]], axis=0)
    two = ring(one, 1)
    three = ring(two, 1)
    cols = ((1,), (1,))
    hiddens, d_gates, d_ups, x_parts, dy_parts = [], [], [], [], []

    def work(x_rows, dy_rows):
        gate_pre = dot(x_rows, wg, cols)
        up_pre = dot(x_rows, wu, cols)
        sig_gate = jax.nn.sigmoid(gate_pre)
        silu_gate = gate_pre * sig_gate
        hiddens.append((silu_gate * up_pre).astype(BF))
        d_hidden = dot(dy_rows, wd, cols)
        d_gate = (d_hidden * up_pre * sig_gate * (1.0 + gate_pre * (1.0 - sig_gate))).astype(BF)
        d_up = (d_hidden * silu_gate).astype(BF)
        d_gates.append(d_gate)
        d_ups.append(d_up)
        x_parts.append(x_rows)
        dy_parts.append(dy_rows)
        return dot(d_gate, wg) + dot(d_up, wu)

    terms_one = work(one[: 2 * near], one[2 * near :])
    terms_two = work(
        jnp.concatenate([two[: 2 * near], packet[:near]], axis=0),
        jnp.concatenate([two[2 * near :], packet[near:]], axis=0),
    )
    terms_two, terms_own = terms_two[: 2 * near], terms_two[2 * near :]
    one_home = ring(terms_one.astype(BF), -1)
    four = jnp.concatenate([three[:near], three[2 * near : 3 * near]], axis=0)
    four = ring(four + one_home[:1] * 0, 1)
    terms_three = work(three[: 2 * near], three[2 * near :])
    terms_four = work(four[:near], four[near:])

    first = terms_four[:1].astype(BF) * 0
    x_all = jnp.concatenate([*x_parts[:-1], x_parts[-1] + first], axis=0)
    dy_all = jnp.concatenate([*dy_parts[:-1], dy_parts[-1] + first], axis=0)
    rows = ((0,), (0,))
    grads = [
        dot(jnp.concatenate(d_gates, axis=0), x_all, rows),
        dot(jnp.concatenate(d_ups, axis=0), x_all, rows),
        dot(jnp.concatenate(hiddens, axis=0), dy_all, rows),
    ]
    received = [lax.ppermute(grad[PAD:].astype(BF), "core", SWAP) for grad in grads]

    three_near = ring(terms_three.astype(BF), -1)
    four_near = ring(terms_four.astype(BF), -2)
    home_b = terms_two[near:] + three_near[near:].astype(F32)
    home_b = ring(home_b.astype(BF), -2, cross=True)
    home_a = terms_two[:near] + three_near[:near].astype(F32) + four_near.astype(F32)
    home_a = ring(home_a.astype(BF), -2)
    one_across = lax.ppermute(one_home[near:] + three_near[:1] * 0, "core", SWAP)
    summed = terms_own
    for came in (one_home[:near], one_across, home_b, home_a):
        summed = summed + came.astype(F32)
    summed = summed.reshape(XH, capacity, XL * Y, -1)
    summed = jnp.transpose(summed, (0, 2, 1, 3)).astype(BF).reshape(XH * XL * Y, capacity, -1)
    summed = lax.all_to_all(summed, ("xh",) + EXPERT, 0, 0, tiled=True)

    outs = [
        (grad[:PAD] + extra.astype(F32))[:hidden_own].astype(BF)[None]
        for grad, extra in zip(grads, received)
    ]

    place = (slot[:, None] == all_slots[None, :]).astype(BF)
    place = place + sum(out[0, 0, 0] * 0 for out in outs)
    grad_tokens = dot(place, summed.reshape(all_slots.shape[0], -1)).astype(BF)
    return (*outs, grad_tokens)


def solution(mesh):
    fine = Mesh(mesh.devices.reshape(Z, XH, CORE, XL, Y), AXES)
    dp = ("z", "xh", "core")
    placed = (
        P(dp, None),
        P(dp, EXPERT),
        P(dp),
        P(dp),
        P(dp),
        P(EXPERT, dp, None),
        P(EXPERT, dp, None),
        P(EXPERT, dp, None),
    )
    return jax.shard_map(
        local,
        mesh=fine,
        in_specs=placed,
        out_specs=(
            P(EXPERT, dp, None),
            P(EXPERT, dp, None),
            P(EXPERT, dp, None),
            P(dp, EXPERT),
        ),
        check_vma=False,
    )
```

```python
import jax
import jax.numpy as jnp
from jax import lax
from jax.sharding import Mesh
from jax.sharding import PartitionSpec as P

BF = jnp.bfloat16
F32 = jnp.float32
Z, XH, CORE, XL, Y = 8, 2, 2, 2, 8
AXES = ("z", "xh", "core", "xl", "y")
EXPERT = ("xl", "y")
PAD = 176
SWAP = [(0, 1), (1, 0)]


def ring(a, step, cross=False):
    pairs = []
    for z in range(Z):
        for c in range(CORE):
            up = step * (1 - 2 * c) * (-1 if cross and step > 0 else 1)
            pairs.append((z * CORE + c, (z + up) % Z * CORE + (c ^ cross)))
    return lax.ppermute(a, ("z", "core"), pairs)


def dot(a, b, dims=((1,), (0,))):
    return lax.dot_general(a, b, (dims, ((), ())), preferred_element_type=F32)


def local(tokens, out_grad, modality, within_route, gate_values, w_gate, w_up, w_down):
    tok_count, width = tokens.shape
    experts_all = XL * Y // 2
    per_modality = experts_all // 2
    capacity = tok_count * 3 // (2 * experts_all)
    hidden_own = w_gate.shape[1]
    position = lax.axis_index(EXPERT)
    own_expert = position // 2
    expert_id = per_modality * modality + within_route
    one_hot = (expert_id[:, None] == jnp.arange(experts_all, dtype=jnp.int32)[None, :]).astype(
        jnp.int32
    )
    before = jnp.cumsum(one_hot, axis=0) - one_hot
    slot_rank = jnp.sum(before * one_hot, axis=1)
    kept = slot_rank < capacity
    slot = jnp.where(kept, expert_id * capacity + slot_rank, -1)
    all_slots = jnp.arange(XH * 2 * experts_all * capacity, dtype=jnp.int32)
    all_slots = all_slots // (2 * capacity) % experts_all * capacity + all_slots % capacity
    select = (slot[None, :] == all_slots[:, None]).astype(BF)
    own_slots = own_expert * capacity + jnp.arange(capacity, dtype=jnp.int32)
    select_own = (slot[None, :] == own_slots[:, None]).astype(BF)

    pad = ((0, PAD - hidden_own), (0, 0))

    own_w = (w_gate[0], w_up[0], w_down[0])
    other_w = [lax.ppermute(w, "core", SWAP) for w in own_w]
    wg, wu, wd = (
        jnp.concatenate([jnp.pad(own, pad), jnp.pad(other, pad)], axis=0)
        for own, other in zip(own_w, other_w)
    )

    x_own = dot(select_own, tokens).astype(BF)
    x_across = lax.ppermute(x_own, "xh", SWAP)
    scaled = (gate_values[:, None] * out_grad.astype(F32)).astype(BF)
    dy_slices = dot(select, scaled).astype(BF).reshape(XH * XL * Y, capacity, -1)
    dy_slices = lax.all_to_all(dy_slices, ("xh",) + EXPERT, 0, 0, tiled=True)
    dy_slices = dy_slices.reshape((XH, XL * Y) + dy_slices.shape[1:])
    dy_near = jnp.transpose(dy_slices, (0, 2, 1, 3)).reshape(2 * capacity, width)
    side = lax.axis_index("xh")
    x_near = jnp.concatenate(
        [jnp.where(side == 0, x_own, x_across), jnp.where(side == 0, x_across, x_own)], axis=0
    )
    near = 2 * capacity
    x_near = x_near + (other_w[0][:1] + other_w[1][:1] + other_w[2][:1]) * 0
    packet = jnp.concatenate([x_near, dy_near], axis=0)
    one = [ring(packet, 1), ring(packet, 1, cross=True)]
    one = jnp.concatenate([one[0][:near], one[1][:near], one[0][near:], one[1][near:]], axis=0)
    two = ring(one, 1)
    three = ring(two, 1)
    cols = ((1,), (1,))
    hiddens, d_gates, d_ups, x_parts, dy_parts = [], [], [], [], []

    def work(x_rows, dy_rows):
        gate_pre = dot(x_rows, wg, cols)
        up_pre = dot(x_rows, wu, cols)
        sig_gate = jax.nn.sigmoid(gate_pre)
        silu_gate = gate_pre * sig_gate
        hiddens.append((silu_gate * up_pre).astype(BF))
        d_hidden = dot(dy_rows, wd, cols)
        d_gate = (d_hidden * up_pre * sig_gate * (1.0 + gate_pre * (1.0 - sig_gate))).astype(BF)
        d_up = (d_hidden * silu_gate).astype(BF)
        d_gates.append(d_gate)
        d_ups.append(d_up)
        x_parts.append(x_rows)
        dy_parts.append(dy_rows)
        return dot(d_gate, wg) + dot(d_up, wu)

    terms_one = work(one[: 2 * near], one[2 * near :])
    terms_two = work(
        jnp.concatenate([two[: 2 * near], packet[:near]], axis=0),
        jnp.concatenate([two[2 * near :], packet[near:]], axis=0),
    )
    terms_two, terms_own = terms_two[: 2 * near], terms_two[2 * near :]
    one_home = ring(terms_one.astype(BF), -1)
    four = jnp.concatenate([three[:near], three[2 * near : 3 * near]], axis=0)
    four = ring(four + one_home[:1] * 0, 1)
    terms_three = work(three[: 2 * near], three[2 * near :])
    terms_four = work(four[:near], four[near:])

    first = terms_four[:1].astype(BF) * 0
    x_all = jnp.concatenate([*x_parts[:-1], x_parts[-1] + first], axis=0)
    dy_all = jnp.concatenate([*dy_parts[:-1], dy_parts[-1] + first], axis=0)
    rows = ((0,), (0,))
    grads = [
        dot(jnp.concatenate(d_gates, axis=0), x_all, rows),
        dot(jnp.concatenate(d_ups, axis=0), x_all, rows),
        dot(jnp.concatenate(hiddens, axis=0), dy_all, rows),
    ]
    received = [lax.ppermute(grad[PAD:].astype(BF), "core", SWAP) for grad in grads]

    one_across = lax.ppermute(one_home[near:], "core", SWAP)
    three_near = ring(terms_three.astype(BF), -1)
    four_near = ring(terms_four.astype(BF), -2)
    home_b = terms_two[near:] + three_near[near:].astype(F32)
    home_b = ring(home_b.astype(BF), -2, cross=True)
    home_a = terms_two[:near] + three_near[:near].astype(F32) + four_near.astype(F32)
    home_a = ring(home_a.astype(BF), -2)
    summed = terms_own
    for came in (one_home[:near], one_across, home_b, home_a):
        summed = summed + came.astype(F32)
    summed = summed.reshape(XH, capacity, XL * Y, -1)
    summed = jnp.transpose(summed, (0, 2, 1, 3)).astype(BF).reshape(XH * XL * Y, capacity, -1)
    summed = lax.all_to_all(summed, ("xh",) + EXPERT, 0, 0, tiled=True)

    outs = [
        (grad[:PAD] + extra.astype(F32))[:hidden_own].astype(BF)[None]
        for grad, extra in zip(grads, received)
    ]

    place = (slot[:, None] == all_slots[None, :]).astype(BF)
    place = place + sum(out[0, 0, 0] * 0 for out in outs)
    grad_tokens = dot(place, summed.reshape(all_slots.shape[0], -1)).astype(BF)
    return (*outs, grad_tokens)


def solution(mesh):
    fine = Mesh(mesh.devices.reshape(Z, XH, CORE, XL, Y), AXES)
    dp = ("z", "xh", "core")
    placed = (
        P(dp, None),
        P(dp, EXPERT),
        P(dp),
        P(dp),
        P(dp),
        P(EXPERT, dp, None),
        P(EXPERT, dp, None),
        P(EXPERT, dp, None),
    )
    return jax.shard_map(
        local,
        mesh=fine,
        in_specs=placed,
        out_specs=(
            P(EXPERT, dp, None),
            P(EXPERT, dp, None),
            P(EXPERT, dp, None),
            P(dp, EXPERT),
        ),
        check_vma=False,
    )
```
